32 devices in a mesh: groups: 2 (over y), phi: 4 (over z), ev: 4 (over x, core).
Axes of the slice: x: 2, y: 2, z: 4, core: 2. Of those that a mesh axis runs over, the one named last changes fastest.
Arguments:
- cell_feats: bfloat16 [8, 1024, 256], P(('groups', 'ev'), 'phi'), parts along dimension 0, may hold values from -3 to 3
- neighbours: int32 [8, 8, 4], P(('groups', 'ev'), 'phi'), parts along dimension 0, may hold values from 0 to 3
- member_cell: int32 [8, 512], P(('groups', 'ev'), 'phi'), parts along dimension 0, may hold values from 0 to 255, as said below
- member_jet: int32 [8, 512, 1], P(('groups', 'ev'), 'phi'), parts along dimension 0, may hold values from 0 to 15, as said below
- cotangent: bfloat16 [8, 1024, 256], P(('groups', 'ev'), 'phi'), parts along dimension 0, may hold values from -3 to 3
- message_weight: bfloat16 [256, 256], replicated, may hold values from -0.375 to 0.375
- query_weight: bfloat16 [256, 256], replicated, may hold values from -4 to 4
- key_weight: bfloat16 [256, 256], replicated, may hold values from -4 to 4
- value_weight: bfloat16 [256, 256], replicated, may hold values from -0.375 to 0.375
- output_weight: bfloat16 [256, 256], replicated, may hold values from -0.375 to 0.375
Outputs:
- out_cells: bfloat16 [8, 1024, 256], P(('groups', 'ev'), 'phi'), parts along dimension 0
- grad_cells: bfloat16 [8, 1024, 256], P(('groups', 'ev'), 'phi'), parts along dimension 0
- grad_message: float32 [512, 256], P('groups'), parts along dimension 0
- grad_query: float32 [512, 256], P('groups'), parts along dimension 0
- grad_key: float32 [512, 256], P('groups'), parts along dimension 0
- grad_value: float32 [512, 256], P('groups'), parts along dimension 0
- grad_output: float32 [512, 256], P('groups'), parts along dimension 0
The draws below stay inside these ranges and needn't reach their ends.
There are 2 independent parts, one for each index of `groups`. The reference program is written for one: setup_inputs(seed, part) draws one part's arguments, and reference() takes and returns one part's arrays. A program takes and returns all parts, laid end to end along the dimension named above; an argument that names none is the same for every part. Nothing has to cross between parts.
Inputs may be any that keep to these rules, and one draw needn't show every extreme that they name: `member_cell`: within one sector's 128 constituents of an event the cells are distinct. `member_jet`: A constituent of sector p belongs to a jet owned by one of the sectors p - 1 to p + 1 on the loop (jet j is owned by sector j // 4). Among one sector's 128 constituents of an event at most 21 belong to one jet, and some jet has exactly 21 of them.
All inputs are finite; a program needn't handle non-finite values.
Results may differ from the reference program's by a relative error of at most 0.0065.
The reference program's roundings to bfloat16 on the way count: a program that leaves them out, or rounds other values in their place, can miss the bound.
Values may be sent and summed in bfloat16 or wider, within the bound.
A program may use at most 64 MiB of HBM per device.

```python
import math
import jax
import jax.numpy as jnp
from jax import lax

WIDTH = 256
HEADS = 8
BLOCK = 128
NBRS = 4
JET_DEV = 4
CELLS_DEV = 256
BLOCKS_DEV = 2
CONS_DEV = 128
REACH = 1
WINDOW = 3
CAP = 21
CELLS = 1024
CONS = 512
EVENTS = 4
N_PHI = 4


def draw_member_cell(key, part):
    count = EVENTS * (CONS // CONS_DEV)
    keys = jax.random.split(jax.random.fold_in(key, 11), count)
    picks = jax.vmap(lambda single: jax.random.permutation(single, CELLS_DEV)[:CONS_DEV])(keys)
    return picks.reshape(EVENTS, CONS).astype(jnp.int32)


def draw_member_jet(key, part):
    sectors = CONS // CONS_DEV
    total = WINDOW * JET_DEV * CAP
    heaviness = jax.random.randint(jax.random.fold_in(key, 31), (EVENTS, sectors * JET_DEV), 1, 5)
    base_key = jax.random.fold_in(key, 37)

    def one_sector(flat_index):
        event_index = flat_index // sectors
        sector = flat_index % sectors
        single = jax.random.fold_in(base_key, flat_index)
        first, second, third = jax.random.split(single, 3)
        slot = jnp.arange(total, dtype=jnp.int32)
        local = slot // CAP
        level = slot % CAP
        owner = (sector + local // JET_DEV - REACH + sectors) % sectors
        jet = owner * JET_DEV + local % JET_DEV
        weight = jnp.take(heaviness[event_index], jet)
        chosen = jax.random.randint(first, (), 0, WINDOW * JET_DEV)
        order_key = jax.random.permutation(second, total).astype(jnp.int32)
        score = jnp.where(local == chosen, order_key - total, level * 4 // weight * total + order_key)
        order = jnp.argsort(score, stable=True)[:CONS_DEV]
        picked = jet[order]
        shuffle = jax.random.permutation(third, CONS_DEV)
        return picked[shuffle]
    flat = jax.vmap(one_sector)(jnp.arange(EVENTS * sectors, dtype=jnp.int32))
    return flat.reshape(EVENTS, CONS, 1).astype(jnp.int32)


def paired_weights(key):
    base_key = jax.random.fold_in(key, 23)
    first, second = jax.random.split(base_key, 2)
    shape = (WIDTH, WIDTH)
    root = WIDTH ** (-0.5)
    query_part = jnp.clip(jax.random.normal(first, shape, jnp.float32), -4.0, 4.0)
    other_part = jnp.clip(jax.random.normal(second, shape, jnp.float32), -4.0, 4.0)
    return (query_part * root, other_part * root)


def draw_query_weight(key, part):
    return paired_weights(key)[0].astype(jnp.bfloat16)


def draw_key_weight(key, part):
    return paired_weights(key)[1].astype(jnp.bfloat16)


def place_ends(drawn, rng, least, high):
    place = [jax.random.randint(jax.random.fold_in(rng, axis), (), 0, length) for axis, length in enumerate(drawn.shape)]
    main_axis = drawn.shape.index(max(drawn.shape))
    neighbour = place[:main_axis] + [(place[main_axis] + 1) % drawn.shape[main_axis]] + place[main_axis + 1:]
    return drawn.at[tuple(place)].set(least).at[tuple(neighbour)].set(high)


def spiked(array, own_key, source, target, blocks, factor):
    owner, partner = [(jnp.arange(array.shape[axis_at]) // (array.shape[axis_at] // blocks)).reshape([-1 if axis == axis_at else 1 for axis in range(array.ndim)]) for axis_at in (source, target)]
    chosen = jax.random.permutation(own_key, blocks)[partner]
    strong = (owner == chosen) | (owner == (partner + blocks // 2) % blocks)
    return jnp.where(strong, factor * array, array)


def shard_levels(rng, dims, shards, smallest, high):
    level, own = 1.0, jax.random.fold_in(rng, 6)
    for axis_at, blocks in shards:
        heights = jnp.exp(jax.random.uniform(jax.random.fold_in(own, axis_at), (blocks,), jnp.float32, smallest / len(shards), high / len(shards)))
        level = level * jnp.repeat(heights, dims[axis_at] // blocks).reshape([-1 if axis == axis_at else 1 for axis in range(len(dims))])
    return level


def centred(rng, extent, deviation, most, cuts=(), held_as=jnp.bfloat16):
    entries = deviation * jax.random.normal(rng, extent, jnp.float32)
    if cuts:
        entries = entries * shard_levels(rng, extent, cuts, -0.22, 0.18)
    return jnp.clip(entries, -most, most).astype(held_as)


def gaussian_with(stream_key, dims, spread, most, pieces, heavy, held_as=jnp.bfloat16):
    array = spread * jax.random.normal(stream_key, dims, jnp.float32)
    if pieces:
        array = array * shard_levels(stream_key, dims, pieces, -0.22, 0.18)
    return jnp.clip(spiked(array, jax.random.fold_in(stream_key, 3), *heavy), -most, most).astype(held_as)


def setup_inputs(seed: int = 0, part: int = 0) -> dict:
    key_list = jax.random.split(jax.random.key(seed), 11)
    part_keys = jax.random.split(jax.random.fold_in(key_list[10], part), 11)
    return {
        "cell_feats": centred(part_keys[0], (EVENTS, CELLS, WIDTH), 0.5, 3.0, ((0, 4), (1, 4))),
        "neighbours": place_ends(jax.random.randint(part_keys[1], (EVENTS, N_PHI * BLOCKS_DEV, NBRS), 0, BLOCKS_DEV + 2), jax.random.fold_in(part_keys[1], 1), 0, (BLOCKS_DEV + 2) - 1).astype(jnp.int32),
        "member_cell": draw_member_cell(jax.random.fold_in(jax.random.fold_in(key_list[10], part), 71), part),
        "member_jet": draw_member_jet(jax.random.fold_in(jax.random.fold_in(key_list[10], part), 71), part),
        "cotangent": gaussian_with(part_keys[4], (EVENTS, CELLS, WIDTH), 0.5, 3.0, ((0, 4), (1, 4)), (1, 2, 4, 2.0)),
        "message_weight": centred(key_list[5], (WIDTH, WIDTH), WIDTH ** -0.5, 0.375),
        "query_weight": draw_query_weight(jax.random.fold_in(key_list[10], 71), part),
        "key_weight": draw_key_weight(jax.random.fold_in(key_list[10], 71), part),
        "value_weight": centred(key_list[8], (WIDTH, WIDTH), WIDTH ** -0.5, 0.375),
        "output_weight": centred(key_list[9], (WIDTH, WIDTH), WIDTH ** -0.5, 0.375),
    }


def silu_slope(values):
    sigmoid = jax.nn.sigmoid(values)
    return sigmoid * (1.0 + values * (1.0 - sigmoid))

def attend_forward(members, present, query_weight, key_weight, value_weight, output_weight):
    jet_count, slot_count, channels = members.shape
    head_size = channels // HEADS
    score_scale = 1.0 / math.sqrt(head_size)
    flat_members = members.reshape(jet_count * slot_count, channels)

    def project(weight):
        result = jnp.dot(flat_members, weight, preferred_element_type=jnp.float32)
        return result.astype(jnp.bfloat16).reshape(jet_count, slot_count, HEADS, head_size)
    queries = project(query_weight)
    keyed = project(key_weight)
    valued = project(value_weight)
    scores = jnp.einsum('jqnd,jknd->jnqk', queries.astype(jnp.float32), keyed.astype(jnp.float32))
    scores = jnp.where(present[:, None, None, :] > 0.5, scores * score_scale, -1e+30)
    largest = lax.optimization_barrier(jnp.max(scores, axis=-1, keepdims=True))
    powers = jnp.exp(scores - largest)
    chances = powers / lax.optimization_barrier(jnp.sum(powers, axis=-1, keepdims=True))
    chances_low = chances.astype(jnp.bfloat16)
    mixture = jnp.einsum('jnqk,jknd->jqnd', chances_low.astype(jnp.float32), valued.astype(jnp.float32))
    mixture = mixture.astype(jnp.bfloat16).reshape(jet_count * slot_count, channels)
    attended = jnp.dot(mixture, output_weight, preferred_element_type=jnp.float32).astype(jnp.bfloat16)
    return (attended.reshape(jet_count, slot_count, channels), (queries, keyed, valued, chances, chances_low, mixture))

def attend_backward(members, saved, upstream, query_weight, key_weight, value_weight, output_weight):
    queries, keyed, valued, chances, chances_low, mixture = saved
    jet_count, slot_count, channels = members.shape
    head_size = channels // HEADS
    score_scale = 1.0 / math.sqrt(head_size)
    flat_members = members.reshape(jet_count * slot_count, channels)
    flat_upstream = upstream.reshape(jet_count * slot_count, channels)
    output_term = jnp.dot(mixture.T, flat_upstream, preferred_element_type=jnp.float32)
    grad_mix = jnp.dot(flat_upstream, output_weight.T, preferred_element_type=jnp.float32)
    grad_mix = grad_mix.astype(jnp.bfloat16).reshape(jet_count, slot_count, HEADS, head_size)
    grad_chances = jnp.einsum('jqnd,jknd->jnqk', grad_mix.astype(jnp.float32), valued.astype(jnp.float32))
    grad_vals = jnp.einsum('jnqk,jqnd->jknd', chances_low.astype(jnp.float32), grad_mix.astype(jnp.float32))
    grad_vals = grad_vals.astype(jnp.bfloat16)
    inner_sum = lax.optimization_barrier(jnp.sum(chances * grad_chances, axis=-1, keepdims=True))
    grad_scores = (chances * (grad_chances - inner_sum) * score_scale).astype(jnp.bfloat16)
    grad_queries = jnp.einsum('jnqk,jknd->jqnd', grad_scores.astype(jnp.float32), keyed.astype(jnp.float32))
    grad_keys = jnp.einsum('jnqk,jqnd->jknd', grad_scores.astype(jnp.float32), queries.astype(jnp.float32))
    flat_queries = grad_queries.astype(jnp.bfloat16).reshape(jet_count * slot_count, channels)
    flat_keys = grad_keys.astype(jnp.bfloat16).reshape(jet_count * slot_count, channels)
    flat_vals = grad_vals.reshape(jet_count * slot_count, channels)
    query_term = jnp.dot(flat_members.T, flat_queries, preferred_element_type=jnp.float32)
    key_term = jnp.dot(flat_members.T, flat_keys, preferred_element_type=jnp.float32)
    value_term = jnp.dot(flat_members.T, flat_vals, preferred_element_type=jnp.float32)
    grad_members = jnp.dot(flat_queries, query_weight.T, preferred_element_type=jnp.float32)
    grad_members = grad_members + jnp.dot(flat_keys, key_weight.T, preferred_element_type=jnp.float32)
    grad_members = grad_members + jnp.dot(flat_vals, value_weight.T, preferred_element_type=jnp.float32)
    grad_members = grad_members.astype(jnp.bfloat16).reshape(jet_count, slot_count, channels)
    return (grad_members, (query_term, key_term, value_term, output_term))

def reference(cell_feats, neighbours, member_cell, member_jet, cotangent, message_weight, query_weight, key_weight, value_weight, output_weight):
    events, total_cells, channels = cell_feats.shape
    sectors = N_PHI
    per_device = total_cells // sectors
    blocks = per_device // BLOCK
    members_dev = member_cell.shape[1] // sectors
    jet_count = JET_DEV * sectors
    tiles = cell_feats.reshape(events, sectors, blocks, BLOCK, channels)
    extended = jnp.concatenate([jnp.roll(tiles[:, :, blocks - 1:], 1, axis=1), tiles, jnp.roll(tiles[:, :, :1], -1, axis=1)], axis=2)
    pattern = neighbours.reshape(events, sectors, blocks, NBRS)
    counts = lax.optimization_barrier(jnp.sum((pattern[..., None] == jnp.arange(blocks + 2, dtype=jnp.int32)).astype(jnp.float32), axis=3))
    gathered = jnp.einsum('epbj,epjch->epbch', counts, extended.astype(jnp.float32)) * (1.0 / NBRS)
    flat_gathered = gathered.astype(jnp.bfloat16).reshape(-1, channels)
    before_act = jnp.dot(flat_gathered, message_weight, preferred_element_type=jnp.float32)
    hidden = (cell_feats.reshape(-1, channels).astype(jnp.float32) + jax.nn.silu(before_act)).astype(jnp.bfloat16)
    hidden = hidden.reshape(events, sectors, per_device, channels)
    local_cells = member_cell.reshape(events, sectors, members_dev)
    jet_ids = member_jet.reshape(events, sectors, members_dev)
    onehot = (jet_ids[..., None] == jnp.arange(jet_count, dtype=jnp.int32)).astype(jnp.int32)
    ranks = lax.optimization_barrier(jnp.sum((jnp.cumsum(onehot, axis=2) - onehot) * onehot, axis=3)).astype(jnp.int32)
    event_index = jnp.arange(events, dtype=jnp.int32)[:, None, None]
    sector_index = jnp.arange(sectors, dtype=jnp.int32)[None, :, None]
    owner = jet_ids // JET_DEV
    offset_slot = ((sector_index - owner + REACH + sectors) % sectors).astype(jnp.int32)
    chosen = jnp.take_along_axis(hidden, local_cells[..., None], axis=2)
    cot_cells = cotangent.reshape(events, sectors, per_device, channels)
    cot_chosen = jnp.take_along_axis(cot_cells, local_cells[..., None], axis=2)
    empty_slots = jnp.zeros((events, jet_count, WINDOW, CAP, channels), jnp.bfloat16)
    slot_rows = empty_slots.at[event_index, jet_ids, offset_slot, ranks].set(chosen)
    slot_grads = empty_slots.at[event_index, jet_ids, offset_slot, ranks].set(cot_chosen)
    slot_mask = jnp.zeros((events, jet_count, WINDOW, CAP), jnp.float32).at[event_index, jet_ids, offset_slot, ranks].set(1.0)
    owners = events * sectors
    slot_count = WINDOW * CAP
    items = (slot_rows.reshape(owners, JET_DEV, slot_count, channels), slot_mask.reshape(owners, JET_DEV, slot_count), slot_grads.reshape(owners, JET_DEV, slot_count, channels))

    def owner_step(carry, item):
        members, present, upstream = item
        attended, saved = attend_forward(members, present, query_weight, key_weight, value_weight, output_weight)
        grad_members, terms = attend_backward(members, saved, upstream, query_weight, key_weight, value_weight, output_weight)
        carry = tuple((old + new for old, new in zip(carry, terms)))
        return (carry, (attended, grad_members))
    zero_grad = jnp.zeros((channels, channels), jnp.float32)
    terms, stacked = lax.scan(owner_step, (zero_grad, zero_grad, zero_grad, zero_grad), items)
    attended_all = stacked[0].reshape(events, jet_count, WINDOW, CAP, channels)
    grads_all = stacked[1].reshape(events, jet_count, WINDOW, CAP, channels)
    attended_rows = attended_all[event_index, jet_ids, offset_slot, ranks]
    grad_rows = grads_all[event_index, jet_ids, offset_slot, ranks]
    zero_cells = jnp.zeros((events, sectors, per_device, channels), jnp.float32)
    placed = zero_cells.at[event_index, sector_index, local_cells].set(attended_rows.astype(jnp.float32))
    placed_grad = zero_cells.at[event_index, sector_index, local_cells].set(grad_rows.astype(jnp.float32))
    out_cells = (hidden.astype(jnp.float32) + placed).astype(jnp.bfloat16).reshape(events, total_cells, channels)
    grad_hidden = cot_cells.astype(jnp.float32) + placed_grad
    grad_before = (grad_hidden.reshape(-1, channels) * silu_slope(before_act)).astype(jnp.bfloat16)
    message_term = jnp.dot(flat_gathered.T, grad_before, preferred_element_type=jnp.float32)
    grad_gathered = jnp.dot(grad_before, message_weight.T, preferred_element_type=jnp.float32).astype(jnp.bfloat16)
    grad_gathered = grad_gathered.reshape(events, sectors, blocks, BLOCK, channels)
    grad_extended = jnp.einsum('epbj,epbch->epjch', counts, grad_gathered.astype(jnp.float32)) * (1.0 / NBRS)
    grad_extended = grad_extended.astype(jnp.bfloat16)
    from_lower = jnp.roll(grad_extended[:, :, blocks + 1:], 1, axis=1).astype(jnp.float32)
    from_upper = jnp.roll(grad_extended[:, :, :1], -1, axis=1).astype(jnp.float32)
    summed = grad_hidden.reshape(events, sectors, blocks, BLOCK, channels) + grad_extended[:, :, 1:blocks + 1].astype(jnp.float32)
    summed = summed.at[:, :, :1].add(from_lower)
    summed = summed.at[:, :, blocks - 1:].add(from_upper)
    grad_cells = summed.astype(jnp.bfloat16).reshape(events, total_cells, channels)
    totals = (message_term,) + tuple(terms)
    squares = jnp.sum(jnp.stack([jnp.sum(matrix * matrix) for matrix in totals]))
    bound = math.sqrt(5.0) * channels
    factor = bound / jnp.maximum(jnp.sqrt(squares), bound)
    return (out_cells, grad_cells, totals[0] * factor, totals[1] * factor, totals[2] * factor, totals[3] * factor, totals[4] * factor)
```

```python
import functools
import math

import jax
import jax.numpy as jnp
from jax import lax
from jax.experimental import pallas as pl
from jax.experimental.pallas import tpu as pltpu
from jax.sharding import PartitionSpec as P

HEADS = 8
BLOCK = 128
NBRS = 4
JET_DEV = 4
TERMS = 4
MESH = pl.DeviceIdType.MESH
BF16 = jnp.bfloat16
F32 = jnp.float32


def contract(a, b, dim_a, dim_b):
    return lax.dot_general(a, b, (((dim_a,), (dim_b,)), ((), ())), preferred_element_type=F32)


def nn(a, b):
    return contract(a, b, 1, 0)


def nt(a, b):
    return contract(a, b, 1, 1)


def tn(a, b):
    return contract(a, b, 0, 0)


def wrapped(value, count):
    value = jnp.where(value >= count, value - count, value)
    return jnp.where(value >= count, value - count, value)


def layer_kernel(
    plan,
    cells,
    nbrs,
    mcell,
    mjet,
    cot,
    wm,
    wq,
    wk,
    wv,
    wo,
    out_cells,
    grad_cells,
    grad_message,
    grad_query,
    grad_key,
    grad_value,
    grad_output,
    edge_in,
    gedge_out,
    gedge_in,
    feat_out,
    feat_in,
    up_out,
    up_in,
    cnt_out,
    cnt_in,
    att_out,
    att_in,
    gmem_out,
    gmem_in,
    send_sem,
    recv_sem,
    *sums,
):
    sectors, ev_count, radius, capacity, fused = plan
    window = 2 * radius + 1
    rows = JET_DEV * capacity
    slots = window * capacity
    per_device, channels = cells.shape[1:]
    blocks = per_device // BLOCK
    cons = mcell.shape[1]
    sector = lax.axis_index("phi")
    ev = lax.axis_index("ev")
    pending = []

    def sector_at(distance):
        return lax.rem(sector + (distance + sectors), sectors)

    def ev_at(distance):
        return lax.rem(ev + distance, ev_count)

    def send(src, dst, **target):
        index = len(pending)
        copy = pltpu.make_async_remote_copy(
            src_ref=src,
            dst_ref=dst,
            send_sem=send_sem.at[index],
            recv_sem=recv_sem.at[index],
            device_id=target,
            device_id_type=MESH,
        )
        copy.start()
        pending.append(copy)
        return copy

    if fused:
        greeted = [{"phi": sector_at(d)} for d in range(1, sectors)]
        greeted += [{"ev": ev_at(d)} for d in range(1, ev_count)]
    else:
        greeted = [{"phi": sector_at(d)} for d in range(-radius, radius + 1) if d]
    barrier = pltpu.get_barrier_semaphore()
    for target in greeted:
        pl.semaphore_signal(barrier, inc=1, device_id=target, device_id_type=MESH)
    pl.semaphore_wait(barrier, len(greeted))

    edges = [
        send(cells.at[0, pl.ds((blocks - 1) * BLOCK, BLOCK)], edge_in.at[0], phi=sector_at(1)),
        send(cells.at[0, pl.ds(0, BLOCK)], edge_in.at[1], phi=sector_at(-1)),
    ]

    jets = mjet[0]
    offset = wrapped((jets >> 2) - sector + (radius + sectors), sectors)
    local_col = offset * JET_DEV + (jets & (JET_DEV - 1))
    up = lax.broadcasted_iota(jnp.int32, (cons, cons), 0)
    across = lax.broadcasted_iota(jnp.int32, (cons, cons), 1)
    local_row = jnp.sum(jnp.where(up == across, local_col, 0), axis=0, keepdims=True)
    same = jnp.where((up < across) & (local_col == local_row), 1, 0)
    target_row = local_row * capacity + jnp.sum(same, axis=0, keepdims=True)
    cell_hot = jnp.where(
        lax.broadcasted_iota(jnp.int32, (per_device, cons), 0) == mcell[...], 1.0, 0.0
    ).astype(BF16)
    slot_hot = jnp.where(
        lax.broadcasted_iota(jnp.int32, (window * rows, cons), 0) == target_row, 1.0, 0.0
    ).astype(BF16)
    slot_cell = nt(slot_hot, cell_hot).astype(BF16)
    cell_slot = nt(cell_hot, slot_hot).astype(BF16)

    def to_slots(source, out_ref, in_ref):
        placed = nn(slot_cell, source).astype(BF16)
        copies = []
        for w in range(window):
            part = placed[w * rows : (w + 1) * rows]
            if w == radius:
                in_ref[w] = part
            else:
                out_ref[w] = part
                copies.append(
                    send(out_ref.at[w], in_ref.at[2 * radius - w], phi=sector_at(w - radius))
                )
        return copies

    local_jet = lax.broadcasted_iota(jnp.int32, (16, cons), 0)
    arriving = to_slots(cot[0], up_out, up_in)
    for w in range(window):
        hit = (local_jet + w * JET_DEV == local_row) & (local_jet < JET_DEV)
        total = jnp.sum(jnp.where(hit, 1.0, 0.0), axis=1, keepdims=True)
        total = jnp.broadcast_to(total, (16, 128)).astype(BF16)
        if w == radius:
            cnt_in[w] = total
        else:
            cnt_out[w] = total
            arriving.append(
                send(cnt_out.at[w], cnt_in.at[2 * radius - w], phi=sector_at(w - radius))
            )

    counts = [
        [
            sum(jnp.where(nbrs[0, b, k] == j, 1.0, 0.0) for k in range(NBRS)) * (1.0 / NBRS)
            for j in range(blocks + 2)
        ]
        for b in range(blocks)
    ]
    for copy in edges:
        copy.wait_recv()
    extended = [edge_in[0].astype(F32)]
    extended += [cells[0, b * BLOCK : (b + 1) * BLOCK].astype(F32) for b in range(blocks)]
    extended += [edge_in[1].astype(F32)]
    gathered = jnp.concatenate(
        [sum(counts[b][j] * extended[j] for j in range(blocks + 2)) for b in range(blocks)],
        axis=0,
    ).astype(BF16)
    before_act = nn(gathered, wm[...])
    sigmoid = 1.0 / (1.0 + jnp.exp(-before_act))
    hidden = (cells[0].astype(F32) + before_act * sigmoid).astype(BF16)
    slope = sigmoid * (1.0 + before_act * (1.0 - sigmoid))
    features = to_slots(hidden, feat_out, feat_in)

    def by_jet(in_ref):
        parts = [in_ref[v].astype(F32) for v in range(window)]
        return jnp.concatenate(
            [
                parts[v][j * capacity : (j + 1) * capacity]
                for j in range(JET_DEV)
                for v in range(window)
            ],
            axis=0,
        ).astype(BF16)

    def back(rows_by_jet, out_ref, in_ref):
        copies = []
        for v in [v for v in range(window) if v != radius] + [radius]:
            part = jnp.concatenate(
                [
                    rows_by_jet[j * slots + v * capacity : j * slots + (v + 1) * capacity]
                    for j in range(JET_DEV)
                ],
                axis=0,
            ).astype(BF16)
            if v == radius:
                in_ref[v] = part
            else:
                out_ref[v] = part
                copies.append(
                    send(out_ref.at[v], in_ref.at[2 * radius - v], phi=sector_at(v - radius))
                )
        return copies

    for copy in arriving:
        copy.wait_recv()
    upstream = by_jet(up_in)
    grad_mix = nt(upstream, wo[...])
    lane = lax.broadcasted_iota(jnp.int32, (1, slots), 1)
    held = [cnt_in[v].astype(F32) for v in range(window)]
    present = []
    for j in range(JET_DEV):
        limit = jnp.zeros((1, slots), F32)
        for v in range(window):
            inside = (lane >= v * capacity) & (lane < (v + 1) * capacity)
            limit = jnp.where(inside, held[v][j : j + 1, :slots] + float(v * capacity), limit)
        present.append(lane.astype(F32) < limit)

    for copy in features:
        copy.wait_recv()
    members = by_jet(feat_in)
    queries = nn(members, wq[...])
    keyed = nn(members, wk[...])
    valued = nn(members, wv[...])

    head_size = channels // HEADS
    score_scale = 1.0 / math.sqrt(head_size)
    feature = lax.broadcasted_iota(jnp.int32, (slots, channels), 1)
    in_head = [
        (feature >= h * head_size) & (feature < (h + 1) * head_size) for h in range(HEADS)
    ]

    def spread(block):
        return jnp.concatenate(
            [jnp.where(in_head[h], block, 0.0) for h in range(HEADS)], axis=0
        ).astype(BF16)

    def merged(block):
        result = block[:slots]
        for h in range(1, HEADS):
            result = jnp.where(in_head[h], block[h * slots : (h + 1) * slots], result)
        return result

    saved = []
    mixture = []
    for j in range(JET_DEV):
        own = slice(j * slots, (j + 1) * slots)
        query_heads = spread(queries[own])
        keys = keyed[own].astype(BF16)
        vals = valued[own].astype(BF16)
        scores = nt(query_heads, keys)
        scores = jnp.where(present[j], scores * score_scale, -1e30)
        powers = jnp.exp(scores - jnp.max(scores, axis=1, keepdims=True))
        chances = powers * (1.0 / jnp.sum(powers, axis=1, keepdims=True))
        chances_low = chances.astype(BF16)
        mixture.append(merged(nn(chances_low, vals)))
        saved.append((query_heads, keys, vals, chances, chances_low))
    mixture = jnp.concatenate(mixture, axis=0).astype(BF16)
    attended = back(nn(mixture, wo[...]), att_out, att_in)

    grad_queries, grad_keys, grad_vals = [], [], []
    for j in range(JET_DEV):
        own = slice(j * slots, (j + 1) * slots)
        query_heads, keys, vals, chances, chances_low = saved[j]
        mix_heads = spread(grad_mix[own])
        grad_chances = nt(mix_heads, vals)
        grad_vals.append(tn(chances_low, mix_heads))
        inner = jnp.sum(chances * grad_chances, axis=1, keepdims=True)
        grad_scores = (chances * (grad_chances - inner) * score_scale).astype(BF16)
        grad_queries.append(merged(nn(grad_scores, keys)))
        grad_keys.append(tn(grad_scores, query_heads))
    grad_queries = jnp.concatenate(grad_queries, axis=0).astype(BF16)
    grad_keys = jnp.concatenate(grad_keys, axis=0).astype(BF16)
    grad_vals = jnp.concatenate(grad_vals, axis=0).astype(BF16)
    grad_members = nt(grad_queries, wq[...]) + nt(grad_keys, wk[...]) + nt(grad_vals, wv[...])
    returned = back(grad_members, gmem_out, gmem_in)

    terms = [
        tn(members, grad_queries),
        tn(members, grad_keys),
        tn(members, grad_vals),
        tn(mixture, upstream),
    ]

    def put(values, ref):
        flat = ref.shape[2]
        for e in range(ev_count):
            for p in range(sectors):
                first = (e * sectors + p) * flat
                value = values[first // channels]
                first = first % channels
                ref[e, p] = value[first : first + flat].astype(BF16)

    def share_ev(buffers):
        whole, landed = buffers[:2]
        return [
            send(whole.at[ev_at(d)], landed.at[d], ev=ev_at(d)) for d in range(1, ev_count)
        ]

    def share_phi(buffers, copies):
        whole, landed, middle, landed_phi = buffers[:4]
        for copy in copies:
            copy.wait_recv()
        total = whole[ev].astype(F32)
        for d in range(1, ev_count):
            total = total + landed[d].astype(F32)
        middle[...] = total.astype(BF16)
        return [
            send(middle.at[sector_at(d)], landed_phi.at[d], phi=sector_at(d))
            for d in range(1, sectors)
        ]

    def collect_phi(buffers, copies):
        middle, landed_phi, final = buffers[2:]
        for copy in copies:
            copy.wait_recv()
        total = middle[sector].astype(F32)
        for d in range(1, sectors):
            total = total + landed_phi[d].astype(F32)
        final[ev, sector] = total.astype(BF16)
        return [
            send(final.at[ev, sector], final.at[ev, sector], phi=sector_at(d))
            for d in range(1, sectors)
        ]

    def collect_ev(buffers, copies):
        final = buffers[4]
        for copy in copies:
            copy.wait_recv()
        return [send(final.at[ev], final.at[ev], ev=ev_at(d)) for d in range(1, ev_count)]

    if fused:
        first, second = sums[:5], sums[5:]
        put(terms, first[0])
        first_copies = share_ev(first)

    for copy in attended:
        copy.wait_recv()
    all_rows = att_in[...].reshape(window * rows, channels)
    out_cells[0] = (hidden.astype(F32) + nn(cell_slot, all_rows)).astype(BF16)
    for copy in returned:
        copy.wait_recv()
    all_rows = gmem_in[...].reshape(window * rows, channels)
    grad_hidden = cot[0].astype(F32) + nn(cell_slot, all_rows)
    grad_before = (grad_hidden * slope).astype(BF16)
    grad_gathered = nt(grad_before, wm[...]).astype(BF16).astype(F32)
    parts = [grad_gathered[b * BLOCK : (b + 1) * BLOCK] for b in range(blocks)]
    grad_extended = [
        sum(counts[b][j] * parts[b] for b in range(blocks)).astype(BF16)
        for j in range(blocks + 2)
    ]
    gedge_out[0] = grad_extended[blocks + 1]
    gedge_out[1] = grad_extended[0]
    grad_edges = [
        send(gedge_out.at[0], gedge_in.at[0], phi=sector_at(1)),
        send(gedge_out.at[1], gedge_in.at[1], phi=sector_at(-1)),
    ]
    message_term = tn(gathered, grad_before)
    if fused:
        put([message_term], second[0])
        second_copies = share_ev(second)
        first_copies = share_phi(first, first_copies)
    for copy in grad_edges:
        copy.wait_recv()
    for b in range(blocks):
        own = slice(b * BLOCK, (b + 1) * BLOCK)
        block = grad_hidden[own] + grad_extended[b + 1].astype(F32)
        if b == 0:
            block = block + gedge_in[0].astype(F32)
        if b == blocks - 1:
            block = block + gedge_in[1].astype(F32)
        grad_cells[0, own] = block.astype(BF16)

    results = [grad_query, grad_key, grad_value, grad_output]
    if fused:
        second_copies = share_phi(second, second_copies)
        first_copies = collect_phi(first, first_copies)
        second_copies = collect_phi(second, second_copies)
        first_copies = collect_ev(first, first_copies)
        second_copies = collect_ev(second, second_copies)
        for copy in first_copies + second_copies:
            copy.wait_recv()
        squares = jnp.zeros((1, channels), F32)
        for final in (first[4], second[4]):
            flat = final.shape[2]
            for e in range(ev_count):
                for p in range(sectors):
                    value = final[e, p].astype(F32)
                    squares = squares + jnp.sum(value * value, axis=0, keepdims=True)
        squares = jnp.sum(squares, axis=1, keepdims=True)
        bound = math.sqrt(5.0) * channels
        factor = bound / jnp.maximum(jnp.sqrt(squares), bound)
        for final, targets in ((first[4], results), (second[4], [grad_message])):
            flat = final.shape[2]
            for e in range(ev_count):
                for p in range(sectors):
                    start = (e * sectors + p) * flat
                    target = targets[start // channels]
                    start = start % channels
                    target[start : start + flat] = final[e, p].astype(F32) * factor
    else:
        for target, term in zip(results, terms):
            target[...] = term
        grad_message[...] = message_term
    for copy in pending:
        copy.wait_send()


def on_device(sectors, ev_count, *args):
    cell_feats, member_cell = args[0], args[2]
    per_device, channels = cell_feats.shape[1:]
    members_dev = member_cell.shape[1]
    radius = min(4, (sectors - 1) // 2)
    window = 2 * radius + 1
    capacity = max(2, 2 * members_dev // (JET_DEV * window))
    capacity = -(-capacity // 8) * 8
    rows = JET_DEV * capacity
    shares = sectors * ev_count
    fused = channels % (16 * shares) == 0
    copies = 4 + 5 * (window - 1)
    scratch = [pltpu.VMEM((2, BLOCK, channels), BF16) for _ in range(3)]
    scratch += [pltpu.VMEM((window, rows, channels), BF16) for _ in range(4)]
    scratch += [pltpu.VMEM((window, 16, 128), BF16) for _ in range(2)]
    scratch += [pltpu.VMEM((window, rows, channels), BF16) for _ in range(4)]
    sums = []
    if fused:
        copies += 4 * (ev_count - 1) + 4 * (sectors - 1)
        for count in (TERMS, 1):
            flat = count * channels // shares
            sums += [
                pltpu.VMEM((ev_count, sectors, flat, channels), BF16),
                pltpu.VMEM((ev_count, sectors, flat, channels), BF16),
                pltpu.VMEM((sectors, flat, channels), BF16),
                pltpu.VMEM((sectors, flat, channels), BF16),
                pltpu.VMEM((ev_count, sectors, flat, channels), BF16),
            ]
    scratch += [pltpu.SemaphoreType.DMA((copies,)), pltpu.SemaphoreType.DMA((copies,))]
    scratch += sums
    vmem = pl.BlockSpec(memory_space=pltpu.VMEM)
    in_specs = [vmem] * len(args)
    in_specs[1] = pl.BlockSpec(memory_space=pltpu.SMEM)
    cells_out = jax.ShapeDtypeStruct(cell_feats.shape, BF16)
    weight_out = jax.ShapeDtypeStruct((channels, channels), F32)
    outs = pl.pallas_call(
        functools.partial(
            layer_kernel, (sectors, ev_count, radius, capacity, fused)
        ),
        out_shape=[cells_out] * 2 + [weight_out] * 5,
        in_specs=in_specs,
        out_specs=[vmem] * 7,
        scratch_shapes=scratch,
        compiler_params=pltpu.CompilerParams(
            collective_id=0, has_side_effects=True, vmem_limit_bytes=48 * 1024 * 1024
        ),
        name="layer",
    )(*args)
    if fused:
        return tuple(outs)
    totals = lax.psum(tuple(outs[2:]), ("phi", "ev"))
    squares = sum(jnp.sum(matrix * matrix) for matrix in totals)
    bound = math.sqrt(5.0) * channels
    factor = bound / jnp.maximum(jnp.sqrt(squares), bound)
    return tuple(outs[:2]) + tuple(total * factor for total in totals)


def solution(mesh):
    cells = P(("groups", "ev"), "phi", None)
    in_specs = (cells, cells, P(("groups", "ev"), "phi"), cells, cells) + (P(),) * 5
    out_specs = (cells, cells) + (P("groups", None),) * 5
    return jax.shard_map(
        functools.partial(on_device, mesh.shape["phi"], mesh.shape["ev"]),
        mesh=mesh,
        in_specs=in_specs,
        out_specs=out_specs,
        check_vma=False,
    )
```

```python
import functools
import math

import jax
import jax.numpy as jnp
from jax import lax
from jax.experimental import pallas as pl
from jax.experimental.pallas import tpu as pltpu
from jax.sharding import PartitionSpec as P

HEADS = 8
BLOCK = 128
NBRS = 4
JET_DEV = 4
STORES = 4
MESH = pl.DeviceIdType.MESH
BF16 = jnp.bfloat16
F32 = jnp.float32


def contract(a, b, dim_a, dim_b):
    return lax.dot_general(a, b, (((dim_a,), (dim_b,)), ((), ())), preferred_element_type=F32)


def nn(a, b):
    return contract(a, b, 1, 0)


def nt(a, b):
    return contract(a, b, 1, 1)


def tn(a, b):
    return contract(a, b, 0, 0)


def wrapped(value, count):
    value = jnp.where(value >= count, value - count, value)
    return jnp.where(value >= count, value - count, value)


def layer_kernel(
    plan,
    cells_far,
    nbrs_far,
    mcell_far,
    mjet_far,
    cot_far,
    wm_far,
    wq_far,
    wk_far,
    wv_far,
    wo_far,
    out_cells,
    grad_cells,
    grad_message,
    grad_query,
    grad_key,
    grad_value,
    grad_output,
    cells,
    cot,
    wm,
    wq,
    wk,
    wv,
    wo,
    nbrs,
    mcell,
    mjet,
    load_sem,
    edge_in,
    gedge_out,
    gedge_in,
    feat_out,
    feat_in,
    up_out,
    up_in,
    cnt_out,
    cnt_in,
    att_out,
    att_in,
    gmem_out,
    gmem_in,
    send_sem,
    recv_sem,
    *sums,
):
    sectors, ev_count, radius, capacity, fused = plan
    window = 2 * radius + 1
    rows = JET_DEV * capacity
    slots = window * capacity
    per_device, channels = cells.shape[1:]
    blocks = per_device // BLOCK
    cons = mcell.shape[1]
    sector = lax.axis_index("phi")
    ev = lax.axis_index("ev")
    low, high = lax.rem(ev, 2), ev // 2
    low_peer = ev + 1 - 2 * low
    high_peer = ev + 2 - 4 * high
    pending = []

    fetches = {}
    fetched = (
        ("mjet", mjet_far, mjet),
        ("mcell", mcell_far, mcell),
        ("nbrs", nbrs_far, nbrs),
        ("cot", cot_far, cot),
        ("cells", cells_far, cells),
        ("wm", wm_far, wm),
        ("wo", wo_far, wo),
        ("wq", wq_far, wq),
        ("wk", wk_far, wk),
        ("wv", wv_far, wv),
    )
    for index, (name, far, near) in enumerate(fetched):
        fetches[name] = pltpu.make_async_copy(far, near, load_sem.at[index])
        fetches[name].start()

    def sector_at(distance):
        return lax.rem(sector + (distance + sectors), sectors)

    def send(src, dst, **target):
        index = len(pending)
        copy = pltpu.make_async_remote_copy(
            src_ref=src,
            dst_ref=dst,
            send_sem=send_sem.at[index],
            recv_sem=recv_sem.at[index],
            device_id=target,
            device_id_type=MESH,
        )
        copy.start()
        pending.append(copy)
        return copy

    if fused:
        greeted = [{"phi": sector_at(d)} for d in range(1, sectors)]
        greeted += [{"phi": sector_at(d), "ev": high_peer} for d in range(sectors)]
        greeted += [{"ev": low_peer}]
    else:
        greeted = [{"phi": sector_at(d)} for d in range(-radius, radius + 1) if d]
    barrier = pltpu.get_barrier_semaphore()
    for target in greeted:
        pl.semaphore_signal(barrier, inc=1, device_id=target, device_id_type=MESH)
    pl.semaphore_wait(barrier, len(greeted))

    edges = [
        send(cells_far.at[0, pl.ds((blocks - 1) * BLOCK, BLOCK)], edge_in.at[0], phi=sector_at(1)),
        send(cells_far.at[0, pl.ds(0, BLOCK)], edge_in.at[1], phi=sector_at(-1)),
    ]

    for name in ("mjet", "mcell", "nbrs", "cot"):
        fetches[name].wait()
    jets = mjet[...]
    offset = wrapped((jets >> 2) - sector + (radius + sectors), sectors)
    local_row = offset * JET_DEV + (jets & (JET_DEV - 1))
    up = lax.broadcasted_iota(jnp.int32, (cons, cons), 0)
    across = lax.broadcasted_iota(jnp.int32, (cons, cons), 1)
    local_col = jnp.sum(jnp.where(up == across, local_row, 0), axis=1, keepdims=True)
    same = jnp.where((up < across) & (local_col == local_row), 1, 0)
    target_row = local_row * capacity + jnp.sum(same, axis=0, keepdims=True)
    cell_hot = jnp.where(
        lax.broadcasted_iota(jnp.int32, (per_device, cons), 0) == mcell[...], 1.0, 0.0
    ).astype(BF16)
    slot_hot = jnp.where(
        lax.broadcasted_iota(jnp.int32, (window * rows, cons), 0) == target_row, 1.0, 0.0
    ).astype(BF16)
    slot_cell = nt(slot_hot, cell_hot).astype(BF16)
    cell_slot = nt(cell_hot, slot_hot).astype(BF16)

    def to_slots(source, out_ref, in_ref):
        placed = nn(slot_cell, source).astype(BF16)
        copies = []
        for w in range(window):
            part = placed[w * rows : (w + 1) * rows]
            if w == radius:
                in_ref[w] = part
            else:
                out_ref[w] = part
                copies.append(
                    send(out_ref.at[w], in_ref.at[2 * radius - w], phi=sector_at(w - radius))
                )
        return copies

    local_jet = lax.broadcasted_iota(jnp.int32, (16, cons), 0)
    arriving = to_slots(cot[0], up_out, up_in)
    for w in range(window):
        hit = (local_jet + w * JET_DEV == local_row) & (local_jet < JET_DEV)
        total = jnp.sum(jnp.where(hit, 1.0, 0.0), axis=1, keepdims=True)
        total = jnp.broadcast_to(total, (16, 128)).astype(BF16)
        if w == radius:
            cnt_in[w] = total
        else:
            cnt_out[w] = total
            arriving.append(
                send(cnt_out.at[w], cnt_in.at[2 * radius - w], phi=sector_at(w - radius))
            )

    counts = [
        [
            jnp.sum(jnp.where(nbrs[0, b : b + 1] == j, 1.0 / NBRS, 0.0), axis=1, keepdims=True)
            for j in range(blocks + 2)
        ]
        for b in range(blocks)
    ]
    for name in ("cells", "wm", "wo", "wq", "wk", "wv"):
        fetches[name].wait()
    for copy in edges:
        copy.wait_recv()
    extended = [edge_in[0].astype(F32)]
    extended += [cells[0, b * BLOCK : (b + 1) * BLOCK].astype(F32) for b in range(blocks)]
    extended += [edge_in[1].astype(F32)]
    gathered = jnp.concatenate(
        [sum(counts[b][j] * extended[j] for j in range(blocks + 2)) for b in range(blocks)],
        axis=0,
    ).astype(BF16)
    before_act = nn(gathered, wm[...])
    sigmoid = 1.0 / (1.0 + jnp.exp(-before_act))
    hidden = (cells[0].astype(F32) + before_act * sigmoid).astype(BF16)
    slope = sigmoid * (1.0 + before_act * (1.0 - sigmoid))
    features = to_slots(hidden, feat_out, feat_in)

    def by_jet(in_ref):
        parts = [in_ref[v].astype(F32) for v in range(window)]
        return jnp.concatenate(
            [
                parts[v][j * capacity : (j + 1) * capacity]
                for j in range(JET_DEV)
                for v in range(window)
            ],
            axis=0,
        ).astype(BF16)

    def back(rows_by_jet, out_ref, in_ref):
        copies = []
        for v in [v for v in range(window) if v != radius] + [radius]:
            part = jnp.concatenate(
                [
                    rows_by_jet[j * slots + v * capacity : j * slots + (v + 1) * capacity]
                    for j in range(JET_DEV)
                ],
                axis=0,
            ).astype(BF16)
            if v == radius:
                in_ref[v] = part
            else:
                out_ref[v] = part
                copies.append(
                    send(out_ref.at[v], in_ref.at[2 * radius - v], phi=sector_at(v - radius))
                )
        return copies

    for copy in arriving:
        copy.wait_recv()
    upstream = by_jet(up_in)
    grad_mix = nt(upstream, wo[...])
    lane = lax.broadcasted_iota(jnp.int32, (1, slots), 1)
    held = [cnt_in[v].astype(F32) for v in range(window)]
    present = []
    for j in range(JET_DEV):
        limit = jnp.zeros((1, slots), F32)
        for v in range(window):
            inside = (lane >= v * capacity) & (lane < (v + 1) * capacity)
            limit = jnp.where(inside, held[v][j : j + 1, :slots] + float(v * capacity), limit)
        present.append(lane.astype(F32) < limit)

    for copy in features:
        copy.wait_recv()
    members = by_jet(feat_in)
    queries = nn(members, wq[...])
    keyed = nn(members, wk[...])
    valued = nn(members, wv[...])

    head_size = channels // HEADS
    score_scale = 1.0 / math.sqrt(head_size)
    feature = lax.broadcasted_iota(jnp.int32, (slots, channels), 1)
    in_head = [
        (feature >= h * head_size) & (feature < (h + 1) * head_size) for h in range(HEADS)
    ]

    def spread(block):
        return jnp.concatenate(
            [jnp.where(in_head[h], block, 0.0) for h in range(HEADS)], axis=0
        ).astype(BF16)

    def merged(block):
        result = block[:slots]
        for h in range(1, HEADS):
            result = jnp.where(in_head[h], block[h * slots : (h + 1) * slots], result)
        return result

    saved = []
    mixture = []
    for j in range(JET_DEV):
        own = slice(j * slots, (j + 1) * slots)
        query_heads = spread(queries[own])
        keys = keyed[own].astype(BF16)
        vals = valued[own].astype(BF16)
        scores = nt(query_heads, keys)
        scores = jnp.where(present[j], scores * score_scale, -1e30)
        powers = jnp.exp(scores - jnp.max(scores, axis=1, keepdims=True))
        chances = powers * (1.0 / jnp.sum(powers, axis=1, keepdims=True))
        chances_low = chances.astype(BF16)
        mixture.append(merged(nn(chances_low, vals)))
        saved.append((query_heads, keys, vals, chances, chances_low))
    mixture = jnp.concatenate(mixture, axis=0).astype(BF16)
    attended = back(nn(mixture, wo[...]), att_out, att_in)

    def put(values, buffers):
        ref = buffers[0]
        flat = ref.shape[3]
        for c in range(2):
            for x in range(2):
                for p in range(sectors):
                    first = ((c * 2 + x) * sectors + p) * flat
                    value = values[first // channels]
                    first = first % channels
                    ref[c, x, p] = value[first : first + flat].astype(BF16)
        return [send(ref.at[1 - low], buffers[1], ev=low_peer)]

    def landed(copies):
        for copy in copies:
            copy.wait_recv()

    def half(buffers, copies):
        whole, from_low, middle, from_high = buffers[:4]
        landed(copies)
        middle[...] = (whole[low].astype(F32) + from_low[...].astype(F32)).astype(BF16)
        return [send(middle.at[1 - high], from_high, ev=high_peer)]

    def quarter(buffers, copies):
        middle, from_high, share, from_phi = buffers[2:6]
        landed(copies)
        share[...] = (middle[high].astype(F32) + from_high[...].astype(F32)).astype(BF16)
        return [
            send(share.at[sector_at(d)], from_phi.at[d - 1], phi=sector_at(d))
            for d in range(1, sectors)
        ]

    def own_total(buffers, copies):
        share, from_phi, final = buffers[4:]
        landed(copies)
        total = share[sector].astype(F32)
        for d in range(1, sectors):
            total = total + from_phi[d - 1].astype(F32)
        final[low, high, sector] = total.astype(BF16)
        block = final.at[low, high, sector]
        return [send(block, block, phi=sector_at(d)) for d in range(1, sectors)]

    def chips():
        for d in range(1, sectors):
            yield d - 1, sector_at(d), ev, high
        for d in range(sectors):
            yield sectors - 1 + d, sector_at(d), high_peer, 1 - high

    def direct(buffers, copies):
        whole, from_low, middle, from_chips = buffers[:4]
        landed(copies)
        middle[...] = (whole[low].astype(F32) + from_low[...].astype(F32)).astype(BF16)
        return [
            send(middle.at[far_high, far], from_chips.at[index], phi=far, ev=far_ev)
            for index, far, far_ev, far_high in chips()
        ]

    def direct_total(buffers, copies):
        middle, from_chips, final = buffers[2:]
        landed(copies)
        total = middle[high, sector].astype(F32)
        for index in range(2 * sectors - 1):
            total = total + from_chips[index].astype(F32)
        final[low, high, sector] = total.astype(BF16)
        block = final.at[low, high, sector]
        return [send(block, block, phi=far, ev=far_ev) for _, far, far_ev, _ in chips()]

    def redouble_last(buffers, copies):
        landed(copies)
        block = buffers[4].at[low]
        return [send(block, block, ev=low_peer)]

    def double(buffers, copies):
        landed(copies)
        block = buffers[6].at[low, high]
        return [send(block, block, ev=high_peer)]

    def redouble(buffers, copies):
        landed(copies)
        block = buffers[6].at[low]
        return [send(block, block, ev=low_peer)]

    if fused:
        early, late, last = sums[:7], sums[7:14], sums[14:]

    mix_heads = [spread(grad_mix[j * slots : (j + 1) * slots]) for j in range(JET_DEV)]
    grad_vals = jnp.concatenate(
        [tn(saved[j][4], mix_heads[j]) for j in range(JET_DEV)], axis=0
    ).astype(BF16)
    value_term = tn(members, grad_vals)
    output_term = tn(mixture, upstream)
    if fused:
        early_copies = put([value_term, output_term], early)

    grad_queries, grad_keys = [], []
    for j in range(JET_DEV):
        query_heads, keys, vals, chances, chances_low = saved[j]
        grad_chances = nt(mix_heads[j], vals)
        inner = jnp.sum(chances * grad_chances, axis=1, keepdims=True)
        grad_scores = (chances * (grad_chances - inner) * score_scale).astype(BF16)
        grad_queries.append(merged(nn(grad_scores, keys)))
        grad_keys.append(tn(grad_scores, query_heads))
    grad_queries = jnp.concatenate(grad_queries, axis=0).astype(BF16)
    grad_keys = jnp.concatenate(grad_keys, axis=0).astype(BF16)
    grad_members = nt(grad_queries, wq[...]) + nt(grad_keys, wk[...]) + nt(grad_vals, wv[...])
    returned = back(grad_members, gmem_out, gmem_in)
    if fused:
        early_copies = half(early, early_copies)

    query_term = tn(members, grad_queries)
    key_term = tn(members, grad_keys)
    if fused:
        late_copies = put([query_term, key_term], late)
        early_copies = quarter(early, early_copies)
        late_copies = half(late, late_copies)

    for copy in attended:
        copy.wait_recv()
    all_rows = att_in[...].reshape(window * rows, channels)
    out_cells[0] = (hidden.astype(F32) + nn(cell_slot, all_rows)).astype(BF16)
    for copy in returned:
        copy.wait_recv()
    all_rows = gmem_in[...].reshape(window * rows, channels)
    grad_hidden = cot[0].astype(F32) + nn(cell_slot, all_rows)
    grad_before = (grad_hidden * slope).astype(BF16)
    message_term = tn(gathered, grad_before)
    if fused:
        last_copies = put([message_term], last)
    grad_gathered = nt(grad_before, wm[...]).astype(BF16).astype(F32)
    parts = [grad_gathered[b * BLOCK : (b + 1) * BLOCK] for b in range(blocks)]
    grad_extended = [
        sum(counts[b][j] * parts[b] for b in range(blocks)).astype(BF16)
        for j in range(blocks + 2)
    ]
    gedge_out[0] = grad_extended[blocks + 1]
    gedge_out[1] = grad_extended[0]
    grad_edges = [
        send(gedge_out.at[0], gedge_in.at[0], phi=sector_at(1)),
        send(gedge_out.at[1], gedge_in.at[1], phi=sector_at(-1)),
    ]
    if fused:
        early_copies = own_total(early, early_copies)
        last_copies = direct(last, last_copies)
        late_copies = quarter(late, late_copies)
        early_copies = double(early, early_copies)
        last_copies = direct_total(last, last_copies)
        late_copies = own_total(late, late_copies)
    for copy in grad_edges:
        copy.wait_recv()
    for b in range(blocks):
        own = slice(b * BLOCK, (b + 1) * BLOCK)
        block = grad_hidden[own] + grad_extended[b + 1].astype(F32)
        if b == 0:
            block = block + gedge_in[0].astype(F32)
        if b == blocks - 1:
            block = block + gedge_in[1].astype(F32)
        grad_cells[0, own] = block.astype(BF16)

    if fused:
        early_copies = redouble(early, early_copies)
        late_copies = double(late, late_copies)
        last_copies = redouble_last(last, last_copies)
        late_copies = redouble(late, late_copies)
        landed(early_copies + late_copies + last_copies)
        squares = jnp.zeros((1, channels), F32)
        blocks_of = [(c, x, p) for c in range(2) for x in range(2) for p in range(sectors)]
        for buffers in (early, late, last):
            for place in blocks_of:
                value = buffers[-1][place].astype(F32)
                squares = squares + jnp.sum(value * value, axis=0, keepdims=True)
        squares = jnp.sum(squares, axis=1, keepdims=True)
        bound = math.sqrt(5.0) * channels
        factor = bound / jnp.maximum(jnp.sqrt(squares), bound)
        for buffers, targets in (
            (early, [grad_value, grad_output]),
            (late, [grad_query, grad_key]),
            (last, [grad_message]),
        ):
            flat = buffers[-1].shape[3]
            for index, place in enumerate(blocks_of):
                target = targets[index * flat // channels]
                start = index * flat % channels
                target[start : start + flat] = buffers[-1][place].astype(F32) * factor
    else:
        grad_value[...] = value_term
        grad_output[...] = output_term
        grad_query[...] = query_term
        grad_key[...] = key_term
        grad_message[...] = message_term
    for copy in pending:
        copy.wait_send()


def store_kernel(*refs):
    sem = refs[-1]
    copies = []
    for index in range(7):
        near, far = refs[index], refs[7 + index]
        lead = (0,) * (len(near.shape) - 2)
        step = near.shape[-2] // STORES
        for piece in range(STORES):
            place = lead + (pl.ds(piece * step, step),)
            copies.append(
                pltpu.make_async_copy(near.at[place], far.at[place], sem.at[index, piece])
            )
            copies[-1].start()
    for copy in copies:
        copy.wait()


def on_device(sectors, ev_count, *args):
    cell_feats, member_cell = args[0], args[2]
    per_device, channels = cell_feats.shape[1:]
    members_dev = member_cell.shape[1]
    radius = min(4, (sectors - 1) // 2)
    window = 2 * radius + 1
    capacity = max(2, 2 * members_dev // (JET_DEV * window))
    capacity = -(-capacity // 8) * 8
    rows = JET_DEV * capacity
    shares = sectors * ev_count
    fused = ev_count == 4 and channels % (16 * shares) == 0
    copies = 4 + 5 * (window - 1)
    weight = (channels, channels)
    scratch = [pltpu.VMEM(cell_feats.shape, BF16) for _ in range(2)]
    scratch += [pltpu.VMEM(weight, BF16) for _ in range(5)]
    scratch += [pltpu.VMEM(args[1].shape, jnp.int32)]
    scratch += [pltpu.VMEM(member_cell.shape, jnp.int32) for _ in range(2)]
    scratch += [pltpu.SemaphoreType.DMA((10,))]
    scratch += [pltpu.VMEM((2, BLOCK, channels), BF16) for _ in range(3)]
    scratch += [pltpu.VMEM((window, rows, channels), BF16) for _ in range(4)]
    scratch += [pltpu.VMEM((window, 16, 128), BF16) for _ in range(2)]
    scratch += [pltpu.VMEM((window, rows, channels), BF16) for _ in range(4)]
    sums = []
    if fused:
        copies += 2 * (4 + 2 * (sectors - 1)) + 2 + 2 * (2 * sectors - 1)
        grouped = [(2, 2, sectors), (2, sectors), (2, sectors), (sectors,), (sectors,)]
        grouped += [(sectors - 1,), (2, 2, sectors)]
        alone = grouped[:3] + [(2 * sectors - 1,), (2, 2, sectors)]
        for count, leads in ((2, grouped), (2, grouped), (1, alone)):
            flat = count * channels // shares
            sums += [pltpu.VMEM(lead + (flat, channels), BF16) for lead in leads]
    scratch += [pltpu.SemaphoreType.DMA((copies,)), pltpu.SemaphoreType.DMA((copies,))]
    scratch += sums
    vmem = pl.BlockSpec(memory_space=pltpu.VMEM)
    far = pl.BlockSpec(memory_space=pltpu.HBM)
    args = list(args)
    args[3] = args[3].reshape(member_cell.shape)
    args = [pltpu.with_memory_space_constraint(arg, pltpu.HBM) for arg in args]
    cells_out = jax.ShapeDtypeStruct(cell_feats.shape, BF16)
    weight_out = jax.ShapeDtypeStruct((channels, channels), F32)

    def near(out):
        return pltpu.VMEM(out.shape, out.dtype) if fused else out

    outs = pl.pallas_call(
        functools.partial(
            layer_kernel, (sectors, ev_count, radius, capacity, fused)
        ),
        out_shape=[near(cells_out)] * 2 + [near(weight_out)] * 5,
        in_specs=[far] * len(args),
        out_specs=[vmem] * 7,
        scratch_shapes=scratch,
        compiler_params=pltpu.CompilerParams(
            collective_id=0, has_side_effects=True, vmem_limit_bytes=48 * 1024 * 1024
        ),
        name="layer",
    )(*args)
    if fused:
        outs = [pltpu.with_memory_space_constraint(out, pltpu.VMEM) for out in outs]
        return tuple(
            pl.pallas_call(
                store_kernel,
                out_shape=[jax.ShapeDtypeStruct(out.shape, out.dtype) for out in outs],
                in_specs=[vmem] * 7,
                out_specs=[far] * 7,
                scratch_shapes=[pltpu.SemaphoreType.DMA((7, STORES))],
                name="store",
            )(*outs)
        )
    totals = lax.psum(tuple(outs[2:]), ("phi", "ev"))
    squares = sum(jnp.sum(matrix * matrix) for matrix in totals)
    bound = math.sqrt(5.0) * channels
    factor = bound / jnp.maximum(jnp.sqrt(squares), bound)
    return tuple(outs[:2]) + tuple(total * factor for total in totals)


def solution(mesh):
    cells = P(("groups", "ev"), "phi", None)
    in_specs = (cells, cells, P(("groups", "ev"), "phi"), cells, cells) + (P(),) * 5
    out_specs = (cells, cells) + (P("groups", None),) * 5
    return jax.shard_map(
        functools.partial(on_device, mesh.shape["phi"], mesh.shape["ev"]),
        mesh=mesh,
        in_specs=in_specs,
        out_specs=out_specs,
        check_vma=False,
    )
```

```python
import functools
import math

import jax
import jax.numpy as jnp
from jax import lax
from jax.experimental import pallas as pl
from jax.experimental.pallas import tpu as pltpu
from jax.sharding import PartitionSpec as P

HEADS = 8
BLOCK = 128
NBRS = 4
JET_DEV = 4
STORES = 4
MESH = pl.DeviceIdType.MESH
BF16 = jnp.bfloat16
F32 = jnp.float32


def contract(a, b, dim_a, dim_b):
    return lax.dot_general(a, b, (((dim_a,), (dim_b,)), ((), ())), preferred_element_type=F32)


def nn(a, b):
    return contract(a, b, 1, 0)


def nt(a, b):
    return contract(a, b, 1, 1)


def tn(a, b):
    return contract(a, b, 0, 0)


def wrapped(value, count):
    value = jnp.where(value >= count, value - count, value)
    return jnp.where(value >= count, value - count, value)


def layer_kernel(
    plan,
    cells_far,
    nbrs_far,
    mcell_far,
    mjet_far,
    cot_far,
    wm_far,
    wq_far,
    wk_far,
    wv_far,
    wo_far,
    out_cells,
    grad_cells,
    grad_message,
    grad_query,
    grad_key,
    grad_value,
    grad_output,
    cells,
    cot,
    wm,
    wq,
    wk,
    wv,
    wo,
    nbrs,
    mcell,
    mjet,
    load_sem,
    edge_in,
    gedge_out,
    gedge_in,
    feat_out,
    feat_in,
    up_out,
    up_in,
    cnt_out,
    cnt_in,
    att_out,
    att_in,
    gmem_out,
    gmem_in,
    gath_out,
    gath_in,
    send_sem,
    recv_sem,
    *sums,
):
    sectors, ev_count, radius, capacity, fused = plan
    window = 2 * radius + 1
    rows = JET_DEV * capacity
    slots = window * capacity
    per_device, channels = cells.shape[1:]
    blocks = per_device // BLOCK
    cons = mcell.shape[1]
    sector = lax.axis_index("phi")
    ev = lax.axis_index("ev")
    low, high = lax.rem(ev, 2), ev // 2
    low_peer = ev + 1 - 2 * low
    high_peer = ev + 2 - 4 * high
    pending = []

    fetches = {}
    fetched = (
        ("mjet", mjet_far, mjet),
        ("mcell", mcell_far, mcell),
        ("nbrs", nbrs_far, nbrs),
        ("cot", cot_far, cot),
        ("cells", cells_far, cells),
        ("wm", wm_far, wm),
        ("wo", wo_far, wo),
        ("wq", wq_far, wq),
        ("wk", wk_far, wk),
        ("wv", wv_far, wv),
    )
    for index, (name, far, near) in enumerate(fetched):
        fetches[name] = pltpu.make_async_copy(far, near, load_sem.at[index])
        fetches[name].start()

    def sector_at(distance):
        return lax.rem(sector + (distance + sectors), sectors)

    def send(src, dst, **target):
        index = len(pending)
        copy = pltpu.make_async_remote_copy(
            src_ref=src,
            dst_ref=dst,
            send_sem=send_sem.at[index],
            recv_sem=recv_sem.at[index],
            device_id=target,
            device_id_type=MESH,
        )
        copy.start()
        pending.append(copy)
        return copy

    def landed(copies):
        for copy in copies:
            copy.wait_recv()

    if fused:
        greeted = [{"phi": sector_at(d)} for d in range(1, sectors)]
        greeted += [{"ev": high_peer}, {"ev": low_peer}]
    else:
        greeted = [{"phi": sector_at(d)} for d in range(-radius, radius + 1) if d]
    barrier = pltpu.get_barrier_semaphore()
    for target in greeted:
        pl.semaphore_signal(barrier, inc=1, device_id=target, device_id_type=MESH)
    pl.semaphore_wait(barrier, len(greeted))

    edges = [
        send(cells_far.at[0, pl.ds((blocks - 1) * BLOCK, BLOCK)], edge_in.at[0], phi=sector_at(1)),
        send(cells_far.at[0, pl.ds(0, BLOCK)], edge_in.at[1], phi=sector_at(-1)),
    ]

    for name in ("mjet", "mcell", "nbrs", "cot"):
        fetches[name].wait()
    jets = mjet[...]
    offset = wrapped((jets >> 2) - sector + (radius + sectors), sectors)
    local_row = offset * JET_DEV + (jets & (JET_DEV - 1))
    up = lax.broadcasted_iota(jnp.int32, (cons, cons), 0)
    across = lax.broadcasted_iota(jnp.int32, (cons, cons), 1)
    local_col = jnp.sum(jnp.where(up == across, local_row, 0), axis=1, keepdims=True)
    same = jnp.where((up < across) & (local_col == local_row), 1, 0)
    target_row = local_row * capacity + jnp.sum(same, axis=0, keepdims=True)
    cell_hot = jnp.where(
        lax.broadcasted_iota(jnp.int32, (per_device, cons), 0) == mcell[...], 1.0, 0.0
    ).astype(BF16)
    slot_hot = jnp.where(
        lax.broadcasted_iota(jnp.int32, (window * rows, cons), 0) == target_row, 1.0, 0.0
    ).astype(BF16)
    slot_cell = nt(slot_hot, cell_hot).astype(BF16)
    cell_slot = nt(cell_hot, slot_hot).astype(BF16)

    def to_slots(source, out_ref, in_ref):
        placed = nn(slot_cell, source).astype(BF16)
        copies = []
        for w in range(window):
            part = placed[w * rows : (w + 1) * rows]
            if w == radius:
                in_ref[w] = part
            else:
                out_ref[w] = part
                copies.append(
                    send(out_ref.at[w], in_ref.at[2 * radius - w], phi=sector_at(w - radius))
                )
        return copies

    local_jet = lax.broadcasted_iota(jnp.int32, (16, cons), 0)
    counted = []
    for w in range(window):
        hit = (local_jet + w * JET_DEV == local_row) & (local_jet < JET_DEV)
        total = jnp.sum(jnp.where(hit, 1.0, 0.0), axis=1, keepdims=True)
        total = jnp.broadcast_to(total, (16, 128)).astype(BF16)
        if w == radius:
            cnt_in[w] = total
        else:
            cnt_out[w] = total
            counted.append(
                send(cnt_out.at[w], cnt_in.at[2 * radius - w], phi=sector_at(w - radius))
            )

    counts = [
        [
            jnp.sum(jnp.where(nbrs[0, b : b + 1] == j, 1.0 / NBRS, 0.0), axis=1, keepdims=True)
            for j in range(blocks + 2)
        ]
        for b in range(blocks)
    ]
    for name in ("cells", "wm", "wo", "wq", "wk", "wv"):
        fetches[name].wait()
    for copy in edges:
        copy.wait_recv()
    extended = [edge_in[0].astype(F32)]
    extended += [cells[0, b * BLOCK : (b + 1) * BLOCK].astype(F32) for b in range(blocks)]
    extended += [edge_in[1].astype(F32)]
    gathered = jnp.concatenate(
        [sum(counts[b][j] * extended[j] for j in range(blocks + 2)) for b in range(blocks)],
        axis=0,
    ).astype(BF16)
    before_act = nn(gathered, wm[...])
    sigmoid = 1.0 / (1.0 + jnp.exp(-before_act))
    hidden = (cells[0].astype(F32) + before_act * sigmoid).astype(BF16)
    slope = sigmoid * (1.0 + before_act * (1.0 - sigmoid))
    features = to_slots(hidden, feat_out, feat_in)
    upstreams = to_slots(cot[0], up_out, up_in)
    member_gathered = to_slots(gathered, gath_out, gath_in)

    bare = jnp.sum(cell_hot.astype(F32), axis=1, keepdims=True) < 0.5
    bare_grad = jnp.where(bare, cot[0].astype(F32) * slope, 0.0).astype(BF16)
    bare_term = tn(gathered, bare_grad)

    def by_jet(in_ref):
        parts = [in_ref[v].astype(F32) for v in range(window)]
        return jnp.concatenate(
            [
                parts[v][j * capacity : (j + 1) * capacity]
                for j in range(JET_DEV)
                for v in range(window)
            ],
            axis=0,
        ).astype(BF16)

    def back(rows_by_jet, out_ref, in_ref):
        copies = []
        for v in [v for v in range(window) if v != radius] + [radius]:
            part = jnp.concatenate(
                [
                    rows_by_jet[j * slots + v * capacity : j * slots + (v + 1) * capacity]
                    for j in range(JET_DEV)
                ],
                axis=0,
            ).astype(BF16)
            if v == radius:
                in_ref[v] = part
            else:
                out_ref[v] = part
                copies.append(
                    send(out_ref.at[v], in_ref.at[2 * radius - v], phi=sector_at(v - radius))
                )
        return copies

    landed(counted)
    lane = lax.broadcasted_iota(jnp.int32, (1, slots), 1)
    held = [cnt_in[v].astype(F32) for v in range(window)]
    present = []
    for j in range(JET_DEV):
        limit = jnp.zeros((1, slots), F32)
        for v in range(window):
            inside = (lane >= v * capacity) & (lane < (v + 1) * capacity)
            limit = jnp.where(inside, held[v][j : j + 1, :slots] + float(v * capacity), limit)
        present.append(lane.astype(F32) < limit)

    landed(features)
    members = by_jet(feat_in)
    queries = nn(members, wq[...])
    keyed = nn(members, wk[...])
    valued = nn(members, wv[...])

    head_size = channels // HEADS
    score_scale = 1.0 / math.sqrt(head_size)
    feature = lax.broadcasted_iota(jnp.int32, (slots, channels), 1)
    in_head = [
        (feature >= h * head_size) & (feature < (h + 1) * head_size) for h in range(HEADS)
    ]

    def spread(block):
        return jnp.concatenate(
            [jnp.where(in_head[h], block, 0.0) for h in range(HEADS)], axis=0
        ).astype(BF16)

    def merged(block):
        result = block[:slots]
        for h in range(1, HEADS):
            result = jnp.where(in_head[h], block[h * slots : (h + 1) * slots], result)
        return result

    saved = []
    mixture = []
    for j in range(JET_DEV):
        own = slice(j * slots, (j + 1) * slots)
        query_heads = spread(queries[own])
        keys = keyed[own].astype(BF16)
        vals = valued[own].astype(BF16)
        scores = nt(query_heads, keys)
        scores = jnp.where(present[j], scores * score_scale, -1e30)
        powers = jnp.exp(scores - jnp.max(scores, axis=1, keepdims=True))
        chances = powers * (1.0 / jnp.sum(powers, axis=1, keepdims=True))
        chances_low = chances.astype(BF16)
        mixture.append(merged(nn(chances_low, vals)))
        saved.append((query_heads, keys, vals, chances, chances_low))
    mixture = jnp.concatenate(mixture, axis=0).astype(BF16)
    attended = back(nn(mixture, wo[...]), att_out, att_in)

    bits = [low, high, lax.rem(sector, 2), sector // 2]
    peers = [
        {"ev": low_peer},
        {"ev": high_peer},
        {"phi": sector + 1 - 2 * bits[2]},
        {"phi": sector + 2 - 4 * bits[3]},
    ]
    shares = [(a, b, c, d) for a in range(2) for b in range(2) for c in range(2) for d in range(2)]

    def put(values, buffers):
        ref = buffers[0]
        flat = ref.shape[4]
        for index, place in enumerate(shares):
            first = index * flat
            value = values[first // channels]
            first = first % channels
            ref[place] = value[first : first + flat].astype(BF16)
        copies = [send(ref.at[1 - bits[0]], buffers[4], **peers[0])]
        return {"buffers": buffers, "copies": copies, "step": 0}

    def advance(group):
        buffers, step = group["buffers"], group["step"]
        landed(group["copies"])
        final = buffers[8]
        if step < 4:
            total = buffers[step][bits[step]].astype(F32) + buffers[4 + step][...].astype(F32)
        if step < 3:
            held = buffers[step + 1]
            held[...] = total.astype(BF16)
            copy = send(
                held.at[1 - bits[step + 1]], buffers[5 + step], **peers[step + 1]
            )
        else:
            if step == 3:
                final[tuple(bits)] = total.astype(BF16)
            block = final.at[tuple(bits[: 7 - step])]
            copy = send(block, block, **peers[6 - step])
        group["copies"], group["step"] = [copy], step + 1

    if fused:
        early, late, last = sums[:9], sums[9:18], sums[18:]

    landed(upstreams)
    upstream = by_jet(up_in)
    grad_mix = nt(upstream, wo[...])
    mix_heads = [spread(grad_mix[j * slots : (j + 1) * slots]) for j in range(JET_DEV)]
    grad_vals = jnp.concatenate(
        [tn(saved[j][4], mix_heads[j]) for j in range(JET_DEV)], axis=0
    ).astype(BF16)
    value_term = tn(members, grad_vals)
    output_term = tn(mixture, upstream)
    if fused:
        early = put([value_term, output_term], early)

    grad_queries, grad_keys = [], []
    for j in range(JET_DEV):
        query_heads, keys, vals, chances, chances_low = saved[j]
        grad_chances = nt(mix_heads[j], vals)
        inner = jnp.sum(chances * grad_chances, axis=1, keepdims=True)
        grad_scores = (chances * (grad_chances - inner) * score_scale).astype(BF16)
        grad_queries.append(merged(nn(grad_scores, keys)))
        grad_keys.append(tn(grad_scores, query_heads))
    grad_queries = jnp.concatenate(grad_queries, axis=0).astype(BF16)
    grad_keys = jnp.concatenate(grad_keys, axis=0).astype(BF16)
    grad_members = nt(grad_queries, wq[...]) + nt(grad_keys, wk[...]) + nt(grad_vals, wv[...])
    returned = back(grad_members, gmem_out, gmem_in)
    if fused:
        advance(early)

    query_term = tn(members, grad_queries)
    key_term = tn(members, grad_keys)
    if fused:
        late = put([query_term, key_term], late)
    landed(member_gathered)
    rows_gathered = by_jet(gath_in)
    rows_act = nn(rows_gathered, wm[...])
    rows_sigmoid = 1.0 / (1.0 + jnp.exp(-rows_act))
    rows_slope = rows_sigmoid * (1.0 + rows_act * (1.0 - rows_sigmoid))
    rows_grad = upstream.astype(F32) + grad_members.astype(BF16).astype(F32)
    message_term = bare_term + tn(rows_gathered, (rows_grad * rows_slope).astype(BF16))
    if fused:
        last = put([message_term], last)
        for group in (early, late, last):
            advance(group)

    landed(attended)
    all_rows = att_in[...].reshape(window * rows, channels)
    out_cells[0] = (hidden.astype(F32) + nn(cell_slot, all_rows)).astype(BF16)
    if fused:
        for group in (early, late, last):
            advance(group)
    landed(returned)
    all_rows = gmem_in[...].reshape(window * rows, channels)
    grad_hidden = cot[0].astype(F32) + nn(cell_slot, all_rows)
    grad_before = (grad_hidden * slope).astype(BF16)
    grad_gathered = nt(grad_before, wm[...]).astype(BF16).astype(F32)
    parts = [grad_gathered[b * BLOCK : (b + 1) * BLOCK] for b in range(blocks)]
    grad_extended = [
        sum(counts[b][j] * parts[b] for b in range(blocks)).astype(BF16)
        for j in range(blocks + 2)
    ]
    gedge_out[0] = grad_extended[blocks + 1]
    gedge_out[1] = grad_extended[0]
    grad_edges = [
        send(gedge_out.at[0], gedge_in.at[0], phi=sector_at(1)),
        send(gedge_out.at[1], gedge_in.at[1], phi=sector_at(-1)),
    ]
    if fused:
        for _ in range(3):
            for group in (early, late, last):
                advance(group)
    landed(grad_edges)
    for b in range(blocks):
        own = slice(b * BLOCK, (b + 1) * BLOCK)
        block = grad_hidden[own] + grad_extended[b + 1].astype(F32)
        if b == 0:
            block = block + gedge_in[0].astype(F32)
        if b == blocks - 1:
            block = block + gedge_in[1].astype(F32)
        grad_cells[0, own] = block.astype(BF16)

    if fused:
        advance(early)
        for _ in range(2):
            advance(late)
            advance(last)
        landed(early["copies"] + late["copies"] + last["copies"])
        squares = jnp.zeros((1, channels), F32)
        groups = (early, late, last)
        finals = [group["buffers"][8] for group in groups]
        for final in finals:
            for place in shares:
                value = final[place].astype(F32)
                squares = squares + jnp.sum(value * value, axis=0, keepdims=True)
        squares = jnp.sum(squares, axis=1, keepdims=True)
        bound = math.sqrt(5.0) * channels
        factor = bound / jnp.maximum(jnp.sqrt(squares), bound)
        targets = ([grad_value, grad_output], [grad_query, grad_key], [grad_message])
        for final, whole in zip(finals, targets):
            flat = final.shape[4]
            for index, place in enumerate(shares):
                target = whole[index * flat // channels]
                start = index * flat % channels
                target[start : start + flat] = final[place].astype(F32) * factor
    else:
        grad_value[...] = value_term
        grad_output[...] = output_term
        grad_query[...] = query_term
        grad_key[...] = key_term
        grad_message[...] = message_term
    for copy in pending:
        copy.wait_send()


def store_kernel(*refs):
    sem = refs[-1]
    copies = []
    for index in range(7):
        near, far = refs[index], refs[7 + index]
        lead = (0,) * (len(near.shape) - 2)
        step = near.shape[-2] // STORES
        for piece in range(STORES):
            place = lead + (pl.ds(piece * step, step),)
            copies.append(
                pltpu.make_async_copy(near.at[place], far.at[place], sem.at[index, piece])
            )
            copies[-1].start()
    for copy in copies:
        copy.wait()


def on_device(sectors, ev_count, *args):
    cell_feats, member_cell = args[0], args[2]
    per_device, channels = cell_feats.shape[1:]
    members_dev = member_cell.shape[1]
    radius = min(4, (sectors - 1) // 2)
    window = 2 * radius + 1
    capacity = max(2, 2 * members_dev // (JET_DEV * window))
    capacity = -(-capacity // 8) * 8
    rows = JET_DEV * capacity
    shares = sectors * ev_count
    fused = ev_count == 4 and sectors == 4 and channels % (16 * shares) == 0
    copies = 4 + 6 * (window - 1)
    weight = (channels, channels)
    scratch = [pltpu.VMEM(cell_feats.shape, BF16) for _ in range(2)]
    scratch += [pltpu.VMEM(weight, BF16) for _ in range(5)]
    scratch += [pltpu.VMEM(args[1].shape, jnp.int32)]
    scratch += [pltpu.VMEM(member_cell.shape, jnp.int32) for _ in range(2)]
    scratch += [pltpu.SemaphoreType.DMA((10,))]
    scratch += [pltpu.VMEM((2, BLOCK, channels), BF16) for _ in range(3)]
    scratch += [pltpu.VMEM((window, rows, channels), BF16) for _ in range(4)]
    scratch += [pltpu.VMEM((window, 16, 128), BF16) for _ in range(2)]
    scratch += [pltpu.VMEM((window, rows, channels), BF16) for _ in range(6)]
    sums = []
    if fused:
        copies += 3 * 8
        leads = [(2,) * count for count in (4, 3, 2, 1, 3, 2, 1, 0, 4)]
        for count in (2, 2, 1):
            flat = count * channels // shares
            sums += [pltpu.VMEM(lead + (flat, channels), BF16) for lead in leads]
    scratch += [pltpu.SemaphoreType.DMA((copies,)), pltpu.SemaphoreType.DMA((copies,))]
    scratch += sums
    vmem = pl.BlockSpec(memory_space=pltpu.VMEM)
    far = pl.BlockSpec(memory_space=pltpu.HBM)
    args = list(args)
    args[3] = args[3].reshape(member_cell.shape)
    args = [pltpu.with_memory_space_constraint(arg, pltpu.HBM) for arg in args]
    cells_out = jax.ShapeDtypeStruct(cell_feats.shape, BF16)
    weight_out = jax.ShapeDtypeStruct((channels, channels), F32)

    def near(out):
        return pltpu.VMEM(out.shape, out.dtype) if fused else out

    outs = pl.pallas_call(
        functools.partial(
            layer_kernel, (sectors, ev_count, radius, capacity, fused)
        ),
        out_shape=[near(cells_out)] * 2 + [near(weight_out)] * 5,
        in_specs=[far] * len(args),
        out_specs=[vmem] * 7,
        scratch_shapes=scratch,
        compiler_params=pltpu.CompilerParams(
            collective_id=0, has_side_effects=True, vmem_limit_bytes=48 * 1024 * 1024
        ),
        name="layer",
    )(*args)
    if fused:
        outs = [pltpu.with_memory_space_constraint(out, pltpu.VMEM) for out in outs]
        return tuple(
            pl.pallas_call(
                store_kernel,
                out_shape=[jax.ShapeDtypeStruct(out.shape, out.dtype) for out in outs],
                in_specs=[vmem] * 7,
                out_specs=[far] * 7,
                scratch_shapes=[pltpu.SemaphoreType.DMA((7, STORES))],
                name="store",
            )(*outs)
        )
    totals = lax.psum(tuple(outs[2:]), ("phi", "ev"))
    squares = sum(jnp.sum(matrix * matrix) for matrix in totals)
    bound = math.sqrt(5.0) * channels
    factor = bound / jnp.maximum(jnp.sqrt(squares), bound)
    return tuple(outs[:2]) + tuple(total * factor for total in totals)


def solution(mesh):
    cells = P(("groups", "ev"), "phi", None)
    in_specs = (cells, cells, P(("groups", "ev"), "phi"), cells, cells) + (P(),) * 5
    out_specs = (cells, cells) + (P("groups", None),) * 5
    return jax.shard_map(
        functools.partial(on_device, mesh.shape["phi"], mesh.shape["ev"]),
        mesh=mesh,
        in_specs=in_specs,
        out_specs=out_specs,
        check_vma=False,
    )
```

```python
import functools
import math

import jax
import jax.numpy as jnp
from jax import lax
from jax.experimental import pallas as pl
from jax.experimental.pallas import tpu as pltpu
from jax.sharding import PartitionSpec as P

HEADS = 8
BLOCK = 128
NBRS = 4
JET_DEV = 4
STORES = 4
MESH = pl.DeviceIdType.MESH
BF16 = jnp.bfloat16
F32 = jnp.float32


def contract(a, b, dim_a, dim_b):
    return lax.dot_general(a, b, (((dim_a,), (dim_b,)), ((), ())), preferred_element_type=F32)


def nn(a, b):
    return contract(a, b, 1, 0)


def nt(a, b):
    return contract(a, b, 1, 1)


def tn(a, b):
    return contract(a, b, 0, 0)


def wrapped(value, count):
    value = jnp.where(value >= count, value - count, value)
    return jnp.where(value >= count, value - count, value)


def layer_kernel(
    plan,
    cells_far,
    nbrs_far,
    mcell_far,
    mjet_far,
    cot_far,
    wm_far,
    wq_far,
    wk_far,
    wv_far,
    wo_far,
    out_cells,
    grad_cells,
    grad_message,
    grad_query,
    grad_key,
    grad_value,
    grad_output,
    cells,
    cot,
    wm,
    wq,
    wk,
    wv,
    wo,
    nbrs,
    mcell,
    mjet,
    load_sem,
    edge_in,
    gedge_out,
    gedge_in,
    feat_out,
    feat_in,
    up_out,
    up_in,
    cnt_out,
    cnt_in,
    att_out,
    att_in,
    gmem_out,
    gmem_in,
    gath_out,
    gath_in,
    send_sem,
    recv_sem,
    *sums,
):
    sectors, ev_count, radius, capacity, fused = plan
    window = 2 * radius + 1
    rows = JET_DEV * capacity
    slots = window * capacity
    per_device, channels = cells.shape[1:]
    blocks = per_device // BLOCK
    cons = mcell.shape[1]
    sector = lax.axis_index("phi")
    ev = lax.axis_index("ev")
    pending = []

    fetches = {}
    fetched = (
        ("mjet", mjet_far, mjet),
        ("mcell", mcell_far, mcell),
        ("nbrs", nbrs_far, nbrs),
        ("cot", cot_far, cot),
        ("cells", cells_far, cells),
        ("wm", wm_far, wm),
        ("wo", wo_far, wo),
        ("wq", wq_far, wq),
        ("wk", wk_far, wk),
        ("wv", wv_far, wv),
    )
    for index, (name, far, near) in enumerate(fetched):
        fetches[name] = pltpu.make_async_copy(far, near, load_sem.at[index])
        fetches[name].start()

    def sector_at(distance):
        return lax.rem(sector + (distance + sectors), sectors)

    def ev_at(distance):
        return lax.rem(ev + distance, ev_count)

    def send(src, dst, **target):
        index = len(pending)
        copy = pltpu.make_async_remote_copy(
            src_ref=src,
            dst_ref=dst,
            send_sem=send_sem.at[index],
            recv_sem=recv_sem.at[index],
            device_id=target,
            device_id_type=MESH,
        )
        copy.start()
        pending.append(copy)
        return copy

    def landed(copies):
        for copy in copies:
            copy.wait_recv()

    if fused:
        greeted = [{"phi": sector_at(d)} for d in range(1, sectors)]
        greeted += [{"ev": ev_at(d)} for d in range(1, ev_count)]
    else:
        greeted = [{"phi": sector_at(d)} for d in range(-radius, radius + 1) if d]
    barrier = pltpu.get_barrier_semaphore()
    for target in greeted:
        pl.semaphore_signal(barrier, inc=1, device_id=target, device_id_type=MESH)
    pl.semaphore_wait(barrier, len(greeted))

    edges = [
        send(cells_far.at[0, pl.ds((blocks - 1) * BLOCK, BLOCK)], edge_in.at[0], phi=sector_at(1)),
        send(cells_far.at[0, pl.ds(0, BLOCK)], edge_in.at[1], phi=sector_at(-1)),
    ]

    for name in ("mjet", "mcell", "nbrs", "cot"):
        fetches[name].wait()
    jets = mjet[...]
    offset = wrapped((jets >> 2) - sector + (radius + sectors), sectors)
    local_row = offset * JET_DEV + (jets & (JET_DEV - 1))
    up = lax.broadcasted_iota(jnp.int32, (cons, cons), 0)
    across = lax.broadcasted_iota(jnp.int32, (cons, cons), 1)
    local_col = jnp.sum(jnp.where(up == across, local_row, 0), axis=1, keepdims=True)
    same = jnp.where((up < across) & (local_col == local_row), 1, 0)
    target_row = local_row * capacity + jnp.sum(same, axis=0, keepdims=True)
    cell_hot = jnp.where(
        lax.broadcasted_iota(jnp.int32, (per_device, cons), 0) == mcell[...], 1.0, 0.0
    ).astype(BF16)
    slot_hot = jnp.where(
        lax.broadcasted_iota(jnp.int32, (window * rows, cons), 0) == target_row, 1.0, 0.0
    ).astype(BF16)
    slot_cell = nt(slot_hot, cell_hot).astype(BF16)
    cell_slot = nt(cell_hot, slot_hot).astype(BF16)

    def to_slots(source, out_ref, in_ref):
        placed = nn(slot_cell, source).astype(BF16)
        copies = []
        for w in range(window):
            part = placed[w * rows : (w + 1) * rows]
            if w == radius:
                in_ref[w] = part
            else:
                out_ref[w] = part
                copies.append(
                    send(out_ref.at[w], in_ref.at[2 * radius - w], phi=sector_at(w - radius))
                )
        return copies

    local_jet = lax.broadcasted_iota(jnp.int32, (16, cons), 0)
    counted = []
    for w in range(window):
        hit = (local_jet + w * JET_DEV == local_row) & (local_jet < JET_DEV)
        total = jnp.sum(jnp.where(hit, 1.0, 0.0), axis=1, keepdims=True)
        total = jnp.broadcast_to(total, (16, 128)).astype(BF16)
        if w == radius:
            cnt_in[w] = total
        else:
            cnt_out[w] = total
            counted.append(
                send(cnt_out.at[w], cnt_in.at[2 * radius - w], phi=sector_at(w - radius))
            )

    counts = [
        [
            jnp.sum(jnp.where(nbrs[0, b : b + 1] == j, 1.0 / NBRS, 0.0), axis=1, keepdims=True)
            for j in range(blocks + 2)
        ]
        for b in range(blocks)
    ]
    for name in ("cells", "wm", "wo", "wq", "wk", "wv"):
        fetches[name].wait()
    for copy in edges:
        copy.wait_recv()
    extended = [edge_in[0].astype(F32)]
    extended += [cells[0, b * BLOCK : (b + 1) * BLOCK].astype(F32) for b in range(blocks)]
    extended += [edge_in[1].astype(F32)]
    gathered = jnp.concatenate(
        [sum(counts[b][j] * extended[j] for j in range(blocks + 2)) for b in range(blocks)],
        axis=0,
    ).astype(BF16)
    before_act = nn(gathered, wm[...])
    sigmoid = 1.0 / (1.0 + jnp.exp(-before_act))
    hidden = (cells[0].astype(F32) + before_act * sigmoid).astype(BF16)
    slope = sigmoid * (1.0 + before_act * (1.0 - sigmoid))
    features = to_slots(hidden, feat_out, feat_in)
    upstreams = to_slots(cot[0], up_out, up_in)
    member_gathered = to_slots(gathered, gath_out, gath_in)

    bare = jnp.sum(cell_hot.astype(F32), axis=1, keepdims=True) < 0.5
    bare_grad = jnp.where(bare, cot[0].astype(F32) * slope, 0.0).astype(BF16)
    bare_term = tn(gathered, bare_grad)

    def by_jet(in_ref):
        parts = [in_ref[v].astype(F32) for v in range(window)]
        return jnp.concatenate(
            [
                parts[v][j * capacity : (j + 1) * capacity]
                for j in range(JET_DEV)
                for v in range(window)
            ],
            axis=0,
        ).astype(BF16)

    def back(rows_by_jet, out_ref, in_ref):
        copies = []
        for v in [v for v in range(window) if v != radius] + [radius]:
            part = jnp.concatenate(
                [
                    rows_by_jet[j * slots + v * capacity : j * slots + (v + 1) * capacity]
                    for j in range(JET_DEV)
                ],
                axis=0,
            ).astype(BF16)
            if v == radius:
                in_ref[v] = part
            else:
                out_ref[v] = part
                copies.append(
                    send(out_ref.at[v], in_ref.at[2 * radius - v], phi=sector_at(v - radius))
                )
        return copies

    landed(counted)
    lane = lax.broadcasted_iota(jnp.int32, (1, slots), 1)
    held = [cnt_in[v].astype(F32) for v in range(window)]
    present = []
    for j in range(JET_DEV):
        limit = jnp.zeros((1, slots), F32)
        for v in range(window):
            inside = (lane >= v * capacity) & (lane < (v + 1) * capacity)
            limit = jnp.where(inside, held[v][j : j + 1, :slots] + float(v * capacity), limit)
        present.append(lane.astype(F32) < limit)

    landed(features)
    members = by_jet(feat_in)
    queries = nn(members, wq[...])
    keyed = nn(members, wk[...])
    valued = nn(members, wv[...])

    head_size = channels // HEADS
    score_scale = 1.0 / math.sqrt(head_size)
    feature = lax.broadcasted_iota(jnp.int32, (slots, channels), 1)
    in_head = [
        (feature >= h * head_size) & (feature < (h + 1) * head_size) for h in range(HEADS)
    ]

    def spread(block):
        return jnp.concatenate(
            [jnp.where(in_head[h], block, 0.0) for h in range(HEADS)], axis=0
        ).astype(BF16)

    def merged(block):
        result = block[:slots]
        for h in range(1, HEADS):
            result = jnp.where(in_head[h], block[h * slots : (h + 1) * slots], result)
        return result

    saved = []
    mixture = []
    for j in range(JET_DEV):
        own = slice(j * slots, (j + 1) * slots)
        query_heads = spread(queries[own])
        keys = keyed[own].astype(BF16)
        vals = valued[own].astype(BF16)
        scores = nt(query_heads, keys)
        scores = jnp.where(present[j], scores * score_scale, -1e30)
        powers = jnp.exp(scores - jnp.max(scores, axis=1, keepdims=True))
        chances = powers * (1.0 / jnp.sum(powers, axis=1, keepdims=True))
        chances_low = chances.astype(BF16)
        mixture.append(merged(nn(chances_low, vals)))
        saved.append((query_heads, keys, vals, chances, chances_low))
    mixture = jnp.concatenate(mixture, axis=0).astype(BF16)
    attended = back(nn(mixture, wo[...]), att_out, att_in)

    def put(values, buffers):
        ref = buffers[0]
        flat = ref.shape[2]
        piece = math.gcd(flat, channels)
        for e in range(ev_count):
            for p in range(sectors):
                for row in range(0, flat, piece):
                    first = (e * sectors + p) * flat + row
                    value = values[first // channels]
                    first = first % channels
                    ref[e, p, row : row + piece] = value[first : first + piece].astype(BF16)
        return [
            send(ref.at[ev_at(d)], buffers[1].at[d - 1], ev=ev_at(d)) for d in range(1, ev_count)
        ]

    def share_phi(buffers, copies):
        whole, from_ev, middle, from_phi = buffers[:4]
        landed(copies)
        total = whole[ev].astype(F32)
        for d in range(1, ev_count):
            total = total + from_ev[d - 1].astype(F32)
        middle[...] = total.astype(BF16)
        return [
            send(middle.at[sector_at(d)], from_phi.at[d - 1], phi=sector_at(d))
            for d in range(1, sectors)
        ]

    def own_total(buffers, copies):
        middle, from_phi, final = buffers[2:]
        landed(copies)
        total = middle[sector].astype(F32)
        for d in range(1, sectors):
            total = total + from_phi[d - 1].astype(F32)
        final[ev, sector] = total.astype(BF16)
        block = final.at[ev, sector]
        return [send(block, block, phi=sector_at(d)) for d in range(1, sectors)]

    def back_ev(buffers, copies):
        landed(copies)
        block = buffers[4].at[ev]
        return [send(block, block, ev=ev_at(d)) for d in range(1, ev_count)]

    if fused:
        early, late = sums[:5], sums[5:]

    landed(upstreams)
    upstream = by_jet(up_in)
    grad_mix = nt(upstream, wo[...])
    mix_heads = [spread(grad_mix[j * slots : (j + 1) * slots]) for j in range(JET_DEV)]
    grad_vals = jnp.concatenate(
        [tn(saved[j][4], mix_heads[j]) for j in range(JET_DEV)], axis=0
    ).astype(BF16)
    value_term = tn(members, grad_vals)
    output_term = tn(mixture, upstream)
    if fused:
        early_copies = put([value_term, output_term], early)

    grad_queries, grad_keys = [], []
    for j in range(JET_DEV):
        query_heads, keys, vals, chances, chances_low = saved[j]
        grad_chances = nt(mix_heads[j], vals)
        inner = jnp.sum(chances * grad_chances, axis=1, keepdims=True)
        grad_scores = (chances * (grad_chances - inner) * score_scale).astype(BF16)
        grad_queries.append(merged(nn(grad_scores, keys)))
        grad_keys.append(tn(grad_scores, query_heads))
    grad_queries = jnp.concatenate(grad_queries, axis=0).astype(BF16)
    grad_keys = jnp.concatenate(grad_keys, axis=0).astype(BF16)
    grad_members = nt(grad_queries, wq[...]) + nt(grad_keys, wk[...]) + nt(grad_vals, wv[...])
    returned = back(grad_members, gmem_out, gmem_in)
    if fused:
        early_copies = share_phi(early, early_copies)

    query_term = tn(members, grad_queries)
    key_term = tn(members, grad_keys)
    landed(member_gathered)
    rows_gathered = by_jet(gath_in)
    rows_act = nn(rows_gathered, wm[...])
    rows_sigmoid = 1.0 / (1.0 + jnp.exp(-rows_act))
    rows_slope = rows_sigmoid * (1.0 + rows_act * (1.0 - rows_sigmoid))
    rows_grad = upstream.astype(F32) + grad_members.astype(BF16).astype(F32)
    message_term = bare_term + tn(rows_gathered, (rows_grad * rows_slope).astype(BF16))
    if fused:
        late_copies = put([query_term, key_term, message_term], late)
        early_copies = own_total(early, early_copies)

    landed(attended)
    all_rows = att_in[...].reshape(window * rows, channels)
    out_cells[0] = (hidden.astype(F32) + nn(cell_slot, all_rows)).astype(BF16)
    if fused:
        late_copies = share_phi(late, late_copies)
        early_copies = back_ev(early, early_copies)
    landed(returned)
    all_rows = gmem_in[...].reshape(window * rows, channels)
    grad_hidden = cot[0].astype(F32) + nn(cell_slot, all_rows)
    grad_before = (grad_hidden * slope).astype(BF16)
    grad_gathered = nt(grad_before, wm[...]).astype(BF16).astype(F32)
    parts = [grad_gathered[b * BLOCK : (b + 1) * BLOCK] for b in range(blocks)]
    grad_extended = [
        sum(counts[b][j] * parts[b] for b in range(blocks)).astype(BF16)
        for j in range(blocks + 2)
    ]
    gedge_out[0] = grad_extended[blocks + 1]
    gedge_out[1] = grad_extended[0]
    grad_edges = [
        send(gedge_out.at[0], gedge_in.at[0], phi=sector_at(1)),
        send(gedge_out.at[1], gedge_in.at[1], phi=sector_at(-1)),
    ]
    if fused:
        late_copies = own_total(late, late_copies)
    landed(grad_edges)
    for b in range(blocks):
        own = slice(b * BLOCK, (b + 1) * BLOCK)
        block = grad_hidden[own] + grad_extended[b + 1].astype(F32)
        if b == 0:
            block = block + gedge_in[0].astype(F32)
        if b == blocks - 1:
            block = block + gedge_in[1].astype(F32)
        grad_cells[0, own] = block.astype(BF16)

    if fused:
        late_copies = back_ev(late, late_copies)
        landed(early_copies + late_copies)
        squares = jnp.zeros((1, channels), F32)
        blocks_of = [(e, p) for e in range(ev_count) for p in range(sectors)]
        for buffers in (early, late):
            for place in blocks_of:
                value = buffers[-1][place].astype(F32)
                squares = squares + jnp.sum(value * value, axis=0, keepdims=True)
        squares = jnp.sum(squares, axis=1, keepdims=True)
        bound = math.sqrt(5.0) * channels
        factor = bound / jnp.maximum(jnp.sqrt(squares), bound)
        for buffers, targets in (
            (early, [grad_value, grad_output]),
            (late, [grad_query, grad_key, grad_message]),
        ):
            flat = buffers[-1].shape[2]
            piece = math.gcd(flat, channels)
            for index, place in enumerate(blocks_of):
                block = buffers[-1][place].astype(F32) * factor
                for row in range(0, flat, piece):
                    start = index * flat + row
                    target = targets[start // channels]
                    start = start % channels
                    target[start : start + piece] = block[row : row + piece]
    else:
        grad_value[...] = value_term
        grad_output[...] = output_term
        grad_query[...] = query_term
        grad_key[...] = key_term
        grad_message[...] = message_term
    for copy in pending:
        copy.wait_send()


def store_kernel(*refs):
    sem = refs[-1]
    copies = []
    for index in range(7):
        near, far = refs[index], refs[7 + index]
        lead = (0,) * (len(near.shape) - 2)
        step = near.shape[-2] // STORES
        for piece in range(STORES):
            place = lead + (pl.ds(piece * step, step),)
            copies.append(
                pltpu.make_async_copy(near.at[place], far.at[place], sem.at[index, piece])
            )
            copies[-1].start()
    for copy in copies:
        copy.wait()


def on_device(sectors, ev_count, *args):
    cell_feats, member_cell = args[0], args[2]
    per_device, channels = cell_feats.shape[1:]
    members_dev = member_cell.shape[1]
    radius = min(4, (sectors - 1) // 2)
    window = 2 * radius + 1
    capacity = max(2, 2 * members_dev // (JET_DEV * window))
    capacity = -(-capacity // 8) * 8
    rows = JET_DEV * capacity
    shares = sectors * ev_count
    fused = channels % (16 * shares) == 0
    copies = 4 + 6 * (window - 1)
    weight = (channels, channels)
    scratch = [pltpu.VMEM(cell_feats.shape, BF16) for _ in range(2)]
    scratch += [pltpu.VMEM(weight, BF16) for _ in range(5)]
    scratch += [pltpu.VMEM(args[1].shape, jnp.int32)]
    scratch += [pltpu.VMEM(member_cell.shape, jnp.int32) for _ in range(2)]
    scratch += [pltpu.SemaphoreType.DMA((10,))]
    scratch += [pltpu.VMEM((2, BLOCK, channels), BF16) for _ in range(3)]
    scratch += [pltpu.VMEM((window, rows, channels), BF16) for _ in range(4)]
    scratch += [pltpu.VMEM((window, 16, 128), BF16) for _ in range(2)]
    scratch += [pltpu.VMEM((window, rows, channels), BF16) for _ in range(6)]
    sums = []
    if fused:
        copies += 4 * (ev_count - 1) + 4 * (sectors - 1)
        leads = [(ev_count, sectors), (ev_count - 1, sectors), (sectors,), (sectors - 1,)]
        leads += [(ev_count, sectors)]
        for count in (2, 3):
            flat = count * channels // shares
            sums += [pltpu.VMEM(lead + (flat, channels), BF16) for lead in leads]
    scratch += [pltpu.SemaphoreType.DMA((copies,)), pltpu.SemaphoreType.DMA((copies,))]
    scratch += sums
    vmem = pl.BlockSpec(memory_space=pltpu.VMEM)
    far = pl.BlockSpec(memory_space=pltpu.HBM)
    args = list(args)
    args[3] = args[3].reshape(member_cell.shape)
    args = [pltpu.with_memory_space_constraint(arg, pltpu.HBM) for arg in args]
    cells_out = jax.ShapeDtypeStruct(cell_feats.shape, BF16)
    weight_out = jax.ShapeDtypeStruct((channels, channels), F32)

    def near(out):
        return pltpu.VMEM(out.shape, out.dtype) if fused else out

    outs = pl.pallas_call(
        functools.partial(
            layer_kernel, (sectors, ev_count, radius, capacity, fused)
        ),
        out_shape=[near(cells_out)] * 2 + [near(weight_out)] * 5,
        in_specs=[far] * len(args),
        out_specs=[vmem] * 7,
        scratch_shapes=scratch,
        compiler_params=pltpu.CompilerParams(
            collective_id=0, has_side_effects=True, vmem_limit_bytes=48 * 1024 * 1024
        ),
        name="layer",
    )(*args)
    if fused:
        outs = [pltpu.with_memory_space_constraint(out, pltpu.VMEM) for out in outs]
        return tuple(
            pl.pallas_call(
                store_kernel,
                out_shape=[jax.ShapeDtypeStruct(out.shape, out.dtype) for out in outs],
                in_specs=[vmem] * 7,
                out_specs=[far] * 7,
                scratch_shapes=[pltpu.SemaphoreType.DMA((7, STORES))],
                name="store",
            )(*outs)
        )
    totals = lax.psum(tuple(outs[2:]), ("phi", "ev"))
    squares = sum(jnp.sum(matrix * matrix) for matrix in totals)
    bound = math.sqrt(5.0) * channels
    factor = bound / jnp.maximum(jnp.sqrt(squares), bound)
    return tuple(outs[:2]) + tuple(total * factor for total in totals)


def solution(mesh):
    cells = P(("groups", "ev"), "phi", None)
    in_specs = (cells, cells, P(("groups", "ev"), "phi"), cells, cells) + (P(),) * 5
    out_specs = (cells, cells) + (P("groups", None),) * 5
    return jax.shard_map(
        functools.partial(on_device, mesh.shape["phi"], mesh.shape["ev"]),
        mesh=mesh,
        in_specs=in_specs,
        out_specs=out_specs,
        check_vma=False,
    )
```

```python
import functools
import math

import jax
import jax.numpy as jnp
from jax import lax
from jax.experimental import pallas as pl
from jax.experimental.pallas import tpu as pltpu
from jax.sharding import PartitionSpec as P

HEADS = 8
BLOCK = 128
NBRS = 4
JET_DEV = 4
STORES = 4
MESH = pl.DeviceIdType.MESH
BF16 = jnp.bfloat16
F32 = jnp.float32


def contract(a, b, dim_a, dim_b):
    return lax.dot_general(a, b, (((dim_a,), (dim_b,)), ((), ())), preferred_element_type=F32)


def nn(a, b):
    return contract(a, b, 1, 0)


def nt(a, b):
    return contract(a, b, 1, 1)


def tn(a, b):
    return contract(a, b, 0, 0)


def wrapped(value, count):
    value = jnp.where(value >= count, value - count, value)
    return jnp.where(value >= count, value - count, value)


def layer_kernel(
    plan,
    cells_far,
    nbrs_far,
    mcell_far,
    mjet_far,
    cot_far,
    wm_far,
    wq_far,
    wk_far,
    wv_far,
    wo_far,
    out_cells,
    grad_cells,
    grad_message,
    grad_query,
    grad_key,
    grad_value,
    grad_output,
    cells,
    cot,
    wm,
    wq,
    wk,
    wv,
    wo,
    nbrs,
    mcell,
    mjet,
    load_sem,
    edge_in,
    gedge_out,
    gedge_in,
    feat_out,
    feat_in,
    up_out,
    up_in,
    cnt_out,
    cnt_in,
    att_out,
    att_in,
    gmem_out,
    gmem_in,
    gath_out,
    gath_in,
    send_sem,
    recv_sem,
    *sums,
):
    sectors, ev_count, radius, capacity, fused = plan
    window = 2 * radius + 1
    rows = JET_DEV * capacity
    slots = window * capacity
    per_device, channels = cells.shape[1:]
    blocks = per_device // BLOCK
    cons = mcell.shape[1]
    sector = lax.axis_index("phi")
    ev = lax.axis_index("ev")
    low, high = lax.rem(ev, 2), ev // 2
    low_peer = ev + 1 - 2 * low
    high_peer = ev + 2 - 4 * high
    pending = []

    fetches = {}
    fetched = (
        ("mjet", mjet_far, mjet),
        ("mcell", mcell_far, mcell),
        ("nbrs", nbrs_far, nbrs),
        ("cot", cot_far, cot),
        ("cells", cells_far, cells),
        ("wm", wm_far, wm),
        ("wo", wo_far, wo),
        ("wq", wq_far, wq),
        ("wk", wk_far, wk),
        ("wv", wv_far, wv),
    )
    for index, (name, far, near) in enumerate(fetched):
        fetches[name] = pltpu.make_async_copy(far, near, load_sem.at[index])
        fetches[name].start()

    def sector_at(distance):
        return lax.rem(sector + (distance + sectors), sectors)

    def send(src, dst, **target):
        index = len(pending)
        copy = pltpu.make_async_remote_copy(
            src_ref=src,
            dst_ref=dst,
            send_sem=send_sem.at[index],
            recv_sem=recv_sem.at[index],
            device_id=target,
            device_id_type=MESH,
        )
        copy.start()
        pending.append(copy)
        return copy

    def landed(copies):
        for copy in copies:
            copy.wait_recv()

    if fused:
        greeted = [{"phi": sector_at(d)} for d in range(1, sectors)]
        greeted += [{"ev": high_peer}, {"ev": low_peer}]
    else:
        greeted = [{"phi": sector_at(d)} for d in range(-radius, radius + 1) if d]
    barrier = pltpu.get_barrier_semaphore()
    for target in greeted:
        pl.semaphore_signal(barrier, inc=1, device_id=target, device_id_type=MESH)
    pl.semaphore_wait(barrier, len(greeted))

    edges = [
        send(cells_far.at[0, pl.ds((blocks - 1) * BLOCK, BLOCK)], edge_in.at[0], phi=sector_at(1)),
        send(cells_far.at[0, pl.ds(0, BLOCK)], edge_in.at[1], phi=sector_at(-1)),
    ]

    for name in ("mjet", "mcell", "nbrs", "cot"):
        fetches[name].wait()
    jets = mjet[...]
    offset = wrapped((jets >> 2) - sector + (radius + sectors), sectors)
    local_row = offset * JET_DEV + (jets & (JET_DEV - 1))
    up = lax.broadcasted_iota(jnp.int32, (cons, cons), 0)
    across = lax.broadcasted_iota(jnp.int32, (cons, cons), 1)
    local_col = jnp.sum(jnp.where(up == across, local_row, 0), axis=1, keepdims=True)
    same = jnp.where((up < across) & (local_col == local_row), 1, 0)
    target_row = local_row * capacity + jnp.sum(same, axis=0, keepdims=True)
    cell_hot = jnp.where(
        lax.broadcasted_iota(jnp.int32, (per_device, cons), 0) == mcell[...], 1.0, 0.0
    ).astype(BF16)
    slot_hot = jnp.where(
        lax.broadcasted_iota(jnp.int32, (window * rows, cons), 0) == target_row, 1.0, 0.0
    ).astype(BF16)
    slot_cell = nt(slot_hot, cell_hot).astype(BF16)
    cell_slot = nt(cell_hot, slot_hot).astype(BF16)

    def to_slots(source, out_ref, in_ref):
        placed = nn(slot_cell, source).astype(BF16)
        copies = []
        for w in range(window):
            part = placed[w * rows : (w + 1) * rows]
            if w == radius:
                in_ref[w] = part
            else:
                out_ref[w] = part
                copies.append(
                    send(out_ref.at[w], in_ref.at[2 * radius - w], phi=sector_at(w - radius))
                )
        return copies

    local_jet = lax.broadcasted_iota(jnp.int32, (16, cons), 0)
    upstreams = to_slots(cot[0], up_out, up_in)
    counted = []
    for w in range(window):
        hit = (local_jet + w * JET_DEV == local_row) & (local_jet < JET_DEV)
        total = jnp.sum(jnp.where(hit, 1.0, 0.0), axis=1, keepdims=True)
        total = jnp.broadcast_to(total, (16, 128)).astype(BF16)
        if w == radius:
            cnt_in[w] = total
        else:
            cnt_out[w] = total
            counted.append(
                send(cnt_out.at[w], cnt_in.at[2 * radius - w], phi=sector_at(w - radius))
            )

    counts = [
        [
            jnp.sum(jnp.where(nbrs[0, b : b + 1] == j, 1.0 / NBRS, 0.0), axis=1, keepdims=True)
            for j in range(blocks + 2)
        ]
        for b in range(blocks)
    ]
    for name in ("cells", "wm", "wo", "wq", "wk", "wv"):
        fetches[name].wait()
    for copy in edges:
        copy.wait_recv()
    extended = [edge_in[0].astype(F32)]
    extended += [cells[0, b * BLOCK : (b + 1) * BLOCK].astype(F32) for b in range(blocks)]
    extended += [edge_in[1].astype(F32)]
    gathered = jnp.concatenate(
        [sum(counts[b][j] * extended[j] for j in range(blocks + 2)) for b in range(blocks)],
        axis=0,
    ).astype(BF16)
    before_act = nn(gathered, wm[...])
    sigmoid = 1.0 / (1.0 + jnp.exp(-before_act))
    hidden = (cells[0].astype(F32) + before_act * sigmoid).astype(BF16)
    slope = sigmoid * (1.0 + before_act * (1.0 - sigmoid))
    features = to_slots(hidden, feat_out, feat_in)
    member_gathered = to_slots(gathered, gath_out, gath_in)

    bare = jnp.sum(cell_hot.astype(F32), axis=1, keepdims=True) < 0.5
    bare_grad = jnp.where(bare, cot[0].astype(F32) * slope, 0.0).astype(BF16)
    bare_term = tn(gathered, bare_grad)

    def by_jet(in_ref):
        parts = [in_ref[v].astype(F32) for v in range(window)]
        return jnp.concatenate(
            [
                parts[v][j * capacity : (j + 1) * capacity]
                for j in range(JET_DEV)
                for v in range(window)
            ],
            axis=0,
        ).astype(BF16)

    def back(rows_by_jet, out_ref, in_ref):
        copies = []
        for v in [v for v in range(window) if v != radius] + [radius]:
            part = jnp.concatenate(
                [
                    rows_by_jet[j * slots + v * capacity : j * slots + (v + 1) * capacity]
                    for j in range(JET_DEV)
                ],
                axis=0,
            ).astype(BF16)
            if v == radius:
                in_ref[v] = part
            else:
                out_ref[v] = part
                copies.append(
                    send(out_ref.at[v], in_ref.at[2 * radius - v], phi=sector_at(v - radius))
                )
        return copies

    landed(counted)
    lane = lax.broadcasted_iota(jnp.int32, (1, slots), 1)
    held = [cnt_in[v].astype(F32) for v in range(window)]
    present = []
    for j in range(JET_DEV):
        limit = jnp.zeros((1, slots), F32)
        for v in range(window):
            inside = (lane >= v * capacity) & (lane < (v + 1) * capacity)
            limit = jnp.where(inside, held[v][j : j + 1, :slots] + float(v * capacity), limit)
        present.append(lane.astype(F32) < limit)

    landed(features)
    members = by_jet(feat_in)
    queries = nn(members, wq[...])
    keyed = nn(members, wk[...])
    valued = nn(members, wv[...])

    head_size = channels // HEADS
    score_scale = 1.0 / math.sqrt(head_size)
    feature = lax.broadcasted_iota(jnp.int32, (slots, channels), 1)
    in_head = [
        (feature >= h * head_size) & (feature < (h + 1) * head_size) for h in range(HEADS)
    ]

    def spread(block):
        return jnp.concatenate(
            [jnp.where(in_head[h], block, 0.0) for h in range(HEADS)], axis=0
        ).astype(BF16)

    def merged(block):
        result = block[:slots]
        for h in range(1, HEADS):
            result = jnp.where(in_head[h], block[h * slots : (h + 1) * slots], result)
        return result

    saved = []
    mixture = []
    for j in range(JET_DEV):
        own = slice(j * slots, (j + 1) * slots)
        query_heads = spread(queries[own])
        keys = keyed[own].astype(BF16)
        vals = valued[own].astype(BF16)
        scores = nt(query_heads, keys)
        scores = jnp.where(present[j], scores * score_scale, -1e30)
        powers = jnp.exp(scores - jnp.max(scores, axis=1, keepdims=True))
        chances = powers * (1.0 / jnp.sum(powers, axis=1, keepdims=True))
        chances_low = chances.astype(BF16)
        mixture.append(merged(nn(chances_low, vals)))
        saved.append((query_heads, keys, vals, chances, chances_low))
    mixture = jnp.concatenate(mixture, axis=0).astype(BF16)
    attended = back(nn(mixture, wo[...]), att_out, att_in)

    def put(values, buffers):
        ref = buffers[0]
        flat = ref.shape[3]
        piece = math.gcd(flat, channels)
        for c in range(2):
            for x in range(2):
                for p in range(sectors):
                    for row in range(0, flat, piece):
                        first = ((c * 2 + x) * sectors + p) * flat + row
                        value = values[first // channels]
                        first = first % channels
                        ref[c, x, p, row : row + piece] = value[first : first + piece].astype(BF16)
        return [send(ref.at[1 - low], buffers[1], ev=low_peer)]

    def half(buffers, copies):
        whole, from_low, middle, from_high = buffers[:4]
        landed(copies)
        middle[...] = (whole[low].astype(F32) + from_low[...].astype(F32)).astype(BF16)
        return [send(middle.at[1 - high], from_high, ev=high_peer)]

    def quarter(buffers, copies):
        middle, from_high, share, from_phi = buffers[2:6]
        landed(copies)
        share[...] = (middle[high].astype(F32) + from_high[...].astype(F32)).astype(BF16)
        return [
            send(share.at[sector_at(d)], from_phi.at[d - 1], phi=sector_at(d))
            for d in range(1, sectors)
        ]

    def own_total(buffers, copies):
        share, from_phi, final = buffers[4:]
        landed(copies)
        total = share[sector].astype(F32)
        for d in range(1, sectors):
            total = total + from_phi[d - 1].astype(F32)
        final[low, high, sector] = total.astype(BF16)
        block = final.at[low, high, sector]
        return [send(block, block, phi=sector_at(d)) for d in range(1, sectors)]

    def double(buffers, copies):
        landed(copies)
        block = buffers[6].at[low, high]
        return [send(block, block, ev=high_peer)]

    def redouble(buffers, copies):
        landed(copies)
        block = buffers[6].at[low]
        return [send(block, block, ev=low_peer)]

    if fused:
        early, late = sums[:7], sums[7:]

    landed(upstreams)
    upstream = by_jet(up_in)
    grad_mix = nt(upstream, wo[...])
    mix_heads = [spread(grad_mix[j * slots : (j + 1) * slots]) for j in range(JET_DEV)]
    grad_vals = jnp.concatenate(
        [tn(saved[j][4], mix_heads[j]) for j in range(JET_DEV)], axis=0
    ).astype(BF16)
    value_term = tn(members, grad_vals)
    output_term = tn(mixture, upstream)
    if fused:
        early_copies = put([value_term, output_term], early)

    grad_queries, grad_keys = [], []
    for j in range(JET_DEV):
        query_heads, keys, vals, chances, chances_low = saved[j]
        grad_chances = nt(mix_heads[j], vals)
        inner = jnp.sum(chances * grad_chances, axis=1, keepdims=True)
        grad_scores = (chances * (grad_chances - inner) * score_scale).astype(BF16)
        grad_queries.append(merged(nn(grad_scores, keys)))
        grad_keys.append(tn(grad_scores, query_heads))
    grad_queries = jnp.concatenate(grad_queries, axis=0).astype(BF16)
    grad_keys = jnp.concatenate(grad_keys, axis=0).astype(BF16)
    grad_members = nt(grad_queries, wq[...]) + nt(grad_keys, wk[...]) + nt(grad_vals, wv[...])
    returned = back(grad_members, gmem_out, gmem_in)
    if fused:
        early_copies = half(early, early_copies)

    query_term = tn(members, grad_queries)
    key_term = tn(members, grad_keys)
    landed(member_gathered)
    rows_gathered = by_jet(gath_in)
    rows_act = nn(rows_gathered, wm[...])
    rows_sigmoid = 1.0 / (1.0 + jnp.exp(-rows_act))
    rows_slope = rows_sigmoid * (1.0 + rows_act * (1.0 - rows_sigmoid))
    rows_grad = upstream.astype(F32) + grad_members.astype(BF16).astype(F32)
    message_term = bare_term + tn(rows_gathered, (rows_grad * rows_slope).astype(BF16))
    if fused:
        late_copies = put([query_term, key_term, message_term], late)
        early_copies = quarter(early, early_copies)
        late_copies = half(late, late_copies)

    landed(attended)
    all_rows = att_in[...].reshape(window * rows, channels)
    out_cells[0] = (hidden.astype(F32) + nn(cell_slot, all_rows)).astype(BF16)
    if fused:
        early_copies = own_total(early, early_copies)
        late_copies = quarter(late, late_copies)
    landed(returned)
    all_rows = gmem_in[...].reshape(window * rows, channels)
    grad_hidden = cot[0].astype(F32) + nn(cell_slot, all_rows)
    grad_before = (grad_hidden * slope).astype(BF16)
    grad_gathered = nt(grad_before, wm[...]).astype(BF16).astype(F32)
    parts = [grad_gathered[b * BLOCK : (b + 1) * BLOCK] for b in range(blocks)]
    grad_extended = [
        sum(counts[b][j] * parts[b] for b in range(blocks)).astype(BF16)
        for j in range(blocks + 2)
    ]
    gedge_out[0] = grad_extended[blocks + 1]
    gedge_out[1] = grad_extended[0]
    grad_edges = [
        send(gedge_out.at[0], gedge_in.at[0], phi=sector_at(1)),
        send(gedge_out.at[1], gedge_in.at[1], phi=sector_at(-1)),
    ]
    if fused:
        early_copies = double(early, early_copies)
        late_copies = own_total(late, late_copies)
        early_copies = redouble(early, early_copies)
    landed(grad_edges)
    for b in range(blocks):
        own = slice(b * BLOCK, (b + 1) * BLOCK)
        block = grad_hidden[own] + grad_extended[b + 1].astype(F32)
        if b == 0:
            block = block + gedge_in[0].astype(F32)
        if b == blocks - 1:
            block = block + gedge_in[1].astype(F32)
        grad_cells[0, own] = block.astype(BF16)

    if fused:
        late_copies = double(late, late_copies)
        late_copies = redouble(late, late_copies)
        landed(early_copies + late_copies)
        squares = jnp.zeros((1, channels), F32)
        blocks_of = [(c, x, p) for c in range(2) for x in range(2) for p in range(sectors)]
        for buffers in (early, late):
            for place in blocks_of:
                value = buffers[-1][place].astype(F32)
                squares = squares + jnp.sum(value * value, axis=0, keepdims=True)
        squares = jnp.sum(squares, axis=1, keepdims=True)
        bound = math.sqrt(5.0) * channels
        factor = bound / jnp.maximum(jnp.sqrt(squares), bound)
        for buffers, targets in (
            (early, [grad_value, grad_output]),
            (late, [grad_query, grad_key, grad_message]),
        ):
            flat = buffers[-1].shape[3]
            piece = math.gcd(flat, channels)
            for index, place in enumerate(blocks_of):
                block = buffers[-1][place].astype(F32) * factor
                for row in range(0, flat, piece):
                    start = index * flat + row
                    target = targets[start // channels]
                    start = start % channels
                    target[start : start + piece] = block[row : row + piece]
    else:
        grad_value[...] = value_term
        grad_output[...] = output_term
        grad_query[...] = query_term
        grad_key[...] = key_term
        grad_message[...] = message_term
    for copy in pending:
        copy.wait_send()


def store_kernel(*refs):
    sem = refs[-1]
    copies = []
    for index in range(7):
        near, far = refs[index], refs[7 + index]
        lead = (0,) * (len(near.shape) - 2)
        step = near.shape[-2] // STORES
        for piece in range(STORES):
            place = lead + (pl.ds(piece * step, step),)
            copies.append(
                pltpu.make_async_copy(near.at[place], far.at[place], sem.at[index, piece])
            )
            copies[-1].start()
    for copy in copies:
        copy.wait()


def on_device(sectors, ev_count, *args):
    cell_feats, member_cell = args[0], args[2]
    per_device, channels = cell_feats.shape[1:]
    members_dev = member_cell.shape[1]
    radius = min(4, (sectors - 1) // 2)
    window = 2 * radius + 1
    capacity = max(2, 2 * members_dev // (JET_DEV * window))
    capacity = -(-capacity // 8) * 8
    rows = JET_DEV * capacity
    shares = sectors * ev_count
    fused = ev_count == 4 and channels % (16 * shares) == 0
    copies = 4 + 6 * (window - 1)
    weight = (channels, channels)
    scratch = [pltpu.VMEM(cell_feats.shape, BF16) for _ in range(2)]
    scratch += [pltpu.VMEM(weight, BF16) for _ in range(5)]
    scratch += [pltpu.VMEM(args[1].shape, jnp.int32)]
    scratch += [pltpu.VMEM(member_cell.shape, jnp.int32) for _ in range(2)]
    scratch += [pltpu.SemaphoreType.DMA((10,))]
    scratch += [pltpu.VMEM((2, BLOCK, channels), BF16) for _ in range(3)]
    scratch += [pltpu.VMEM((window, rows, channels), BF16) for _ in range(4)]
    scratch += [pltpu.VMEM((window, 16, 128), BF16) for _ in range(2)]
    scratch += [pltpu.VMEM((window, rows, channels), BF16) for _ in range(6)]
    sums = []
    if fused:
        copies += 2 * (4 + 2 * (sectors - 1))
        leads = [(2, 2, sectors), (2, sectors), (2, sectors), (sectors,), (sectors,)]
        leads += [(sectors - 1,), (2, 2, sectors)]
        for count in (2, 3):
            flat = count * channels // shares
            sums += [pltpu.VMEM(lead + (flat, channels), BF16) for lead in leads]
    scratch += [pltpu.SemaphoreType.DMA((copies,)), pltpu.SemaphoreType.DMA((copies,))]
    scratch += sums
    vmem = pl.BlockSpec(memory_space=pltpu.VMEM)
    far = pl.BlockSpec(memory_space=pltpu.HBM)
    args = list(args)
    args[3] = args[3].reshape(member_cell.shape)
    args = [pltpu.with_memory_space_constraint(arg, pltpu.HBM) for arg in args]
    cells_out = jax.ShapeDtypeStruct(cell_feats.shape, BF16)
    weight_out = jax.ShapeDtypeStruct((channels, channels), F32)

    def near(out):
        return pltpu.VMEM(out.shape, out.dtype) if fused else out

    outs = pl.pallas_call(
        functools.partial(
            layer_kernel, (sectors, ev_count, radius, capacity, fused)
        ),
        out_shape=[near(cells_out)] * 2 + [near(weight_out)] * 5,
        in_specs=[far] * len(args),
        out_specs=[vmem] * 7,
        scratch_shapes=scratch,
        compiler_params=pltpu.CompilerParams(
            collective_id=0, has_side_effects=True, vmem_limit_bytes=48 * 1024 * 1024
        ),
        name="layer",
    )(*args)
    if fused:
        outs = [pltpu.with_memory_space_constraint(out, pltpu.VMEM) for out in outs]
        return tuple(
            pl.pallas_call(
                store_kernel,
                out_shape=[jax.ShapeDtypeStruct(out.shape, out.dtype) for out in outs],
                in_specs=[vmem] * 7,
                out_specs=[far] * 7,
                scratch_shapes=[pltpu.SemaphoreType.DMA((7, STORES))],
                name="store",
            )(*outs)
        )
    totals = lax.psum(tuple(outs[2:]), ("phi", "ev"))
    squares = sum(jnp.sum(matrix * matrix) for matrix in totals)
    bound = math.sqrt(5.0) * channels
    factor = bound / jnp.maximum(jnp.sqrt(squares), bound)
    return tuple(outs[:2]) + tuple(total * factor for total in totals)


def solution(mesh):
    cells = P(("groups", "ev"), "phi", None)
    in_specs = (cells, cells, P(("groups", "ev"), "phi"), cells, cells) + (P(),) * 5
    out_specs = (cells, cells) + (P("groups", None),) * 5
    return jax.shard_map(
        functools.partial(on_device, mesh.shape["phi"], mesh.shape["ev"]),
        mesh=mesh,
        in_specs=in_specs,
        out_specs=out_specs,
        check_vma=False,
    )
```
